32 devices in a mesh: comp: 2 (over x), lat: 4 (over y, core), lon: 4 (over z).
Axes of the slice: x: 2, y: 2, z: 4, core: 2. Of those that a mesh axis runs over, the one named last changes fastest.
Arguments:
- state: float32 [2, 12, 64, 512], P('comp', None, 'lat', 'lon'), may hold values from -6 to 6
- prev_surface: float32 [2, 64, 512], P(None, 'lat', 'lon'), may hold values from -6 to 6
- mixing: float32 [2, 11, 64, 512], P('comp', None, 'lat', 'lon'), may hold values from 0.1 to 3
- velocity: float32 [2, 2, 64, 512], P('comp', None, 'lat', 'lon'), may hold values from -0.3 to 0.3
- coupling: float32 [2, 64, 512], P('comp', 'lat', 'lon'), may hold values from 0.1 to 1
- sea_mask: int32 [2, 64, 512], P('comp', 'lat', 'lon'), may hold values 0 or 1
- interp_index: int32 [2, 4, 64, 512], P('comp', None, 'lat', 'lon'), may hold values from 0 to 2047
- interp_weight: float32 [2, 4, 64, 512], P('comp', None, 'lat', 'lon'), may hold values from 0.05 to 0.45
Outputs:
- new_state: float32 [2, 12, 64, 512], P('comp', None, 'lat', 'lon')
- surface_series: float32 [2, 2, 64, 512], P('comp', None, 'lat', 'lon')
The draws below stay inside these ranges and needn't reach their ends.
Inputs may be any that keep to these rules, and one draw needn't show every extreme that they name: `interp_index`: A tile index, r * 128 + c, of a cell in the same latitude-longitude tile.
All inputs are finite; a program needn't handle non-finite values. No bound on the sum of `sea_mask` on one device may be relied on, other than what follows from the above.
Results may differ from the reference program's by a relative error of at most 0.0001.
Values sent between devices are 32-bit elements; how exact they have to be, the bound alone decides.
A program may use at most 64 MiB of HBM per device.

```python
import math
import jax
import jax.numpy as jnp

LEV = 12
NSTEP = 2
CLAT = 16
CLON = 128
NLAT = 64
NLON = 512
CELLS = 2048
N_LAT = 4
N_LON = 4


def with_ends(values, rng, least, largest):
    longest = values.shape.index(max(values.shape))
    spots = []
    for shift in (0, 1):
        where = [jax.random.randint(jax.random.fold_in(rng, axis), (), 0, length) for axis, length in enumerate(values.shape)]
        where[longest] = (where[longest] + shift) % values.shape[longest]
        spots.append(tuple(where))
    return values.at[spots[0]].set(least).at[spots[1]].set(largest)


def shard_levels(stream_key, dims, shards, smallest, high):
    gain = 1.0
    for position, parts in shards:
        steps = jax.random.uniform(jax.random.fold_in(jax.random.fold_in(stream_key, 6), position), (parts,), jnp.float32, smallest / len(shards), high / len(shards))
        gain = gain * jnp.repeat(jnp.exp(steps), dims[position] // parts).reshape((-1,) + (1,) * (len(dims) - 1 - position))
    return gain


def normal_values(rng, dims, scale, reach, shards=(), dtype=jnp.bfloat16):
    level = shard_levels(rng, dims, shards, -0.22, 0.18) if shards else 1.0
    entries = jax.random.normal(rng, dims, jnp.float32) * scale * level
    return jnp.minimum(jnp.maximum(entries, -reach), reach).astype(dtype)


def setup_inputs(seed: int = 0) -> dict:
    seeds = jax.random.split(jax.random.key(seed), 9)
    return {
        "state": normal_values(seeds[0], (2, LEV, NLAT, NLON), 1.0, 6.0, ((0, 2), (2, 4), (3, 4)), jnp.float32),
        "prev_surface": normal_values(seeds[1], (NSTEP, NLAT, NLON), 1.0, 6.0, ((1, 4), (2, 4)), jnp.float32),
        "mixing": jnp.clip(jnp.exp(math.log(3.0) - 3.4011974 * jax.random.uniform(seeds[2], (2, LEV - 1, NLAT, NLON), jnp.float32) ** shard_levels(seeds[2], (2, LEV - 1, NLAT, NLON), ((0, 2), (2, 4), (3, 4)), -0.2, 0.2)), 0.1, 3.0),
        "velocity": jnp.clip(jax.random.uniform(seeds[3], (2, 2, NLAT, NLON), jnp.float32, -0.3, 0.3) * shard_levels(seeds[3], (2, 2, NLAT, NLON), ((0, 2), (2, 4), (3, 4)), -0.4, 0.0), -0.3, 0.3),
        "coupling": jnp.clip(jnp.exp(math.log(1.0) - 2.3025851 * jax.random.uniform(seeds[4], (2, NLAT, NLON), jnp.float32) ** shard_levels(seeds[4], (2, NLAT, NLON), ((0, 2), (1, 4), (2, 4)), -0.2, 0.2)), 0.1, 1.0),
        "sea_mask": with_ends((jax.random.randint(seeds[5], (2, NLAT, NLON), 0, 3) < 2).astype(jnp.int32), jax.random.fold_in(seeds[5], 1), 0, 1),
        "interp_index": with_ends(jax.random.randint(seeds[6], (2, 4, NLAT, NLON), 0, CELLS), jax.random.fold_in(seeds[6], 1), 0, CELLS - 1).astype(jnp.int32),
        "interp_weight": jnp.clip(0.05 + 0.39999999 * jax.random.uniform(seeds[7], (2, 4, NLAT, NLON), jnp.float32) ** shard_levels(seeds[7], (2, 4, NLAT, NLON), ((0, 2), (2, 4), (3, 4)), -0.2, 0.2), 0.05, 0.45),
    }


smoothing = 0.15


def stencil(field, lat_padded, lon_padded, east_speed, north_speed):
    lat_slope = (lat_padded[:, 0:-4] - 8.0 * lat_padded[:, 1:-3] + 8.0 * lat_padded[:, 3:-1] - lat_padded[:, 4:]) / 12.0
    lon_slope = (lon_padded[:, :, 0:-4] - 8.0 * lon_padded[:, :, 1:-3] + 8.0 * lon_padded[:, :, 3:-1] - lon_padded[:, :, 4:]) / 12.0
    lat_curve = lat_padded[:, 1:-3] + lat_padded[:, 3:-1] - 2.0 * field
    lon_curve = lon_padded[:, :, 1:-3] + lon_padded[:, :, 3:-1] - 2.0 * field
    return field + smoothing * (lat_curve + lon_curve) - east_speed * lon_slope - north_speed * lat_slope


def column_solve(rhs, mixing):
    levels = rhs.shape[0]
    nothing = jnp.zeros_like(rhs[0])
    ratios = []
    values = []
    for level in range(levels):
        lower = mixing[level - 1] if level > 0 else nothing
        upper = mixing[level] if level < levels - 1 else nothing
        pivot = 1.0 + lower + upper
        source = rhs[level]
        if level > 0:
            pivot = pivot + lower * ratios[-1]
            source = source + lower * values[-1]
        ratios.append(-upper / pivot)
        values.append(source / pivot)
    result = [values[-1]]
    for level in range(levels - 2, -1, -1):
        result.insert(0, values[level] - ratios[level] * result[0])
    return jnp.stack(result)


def to_tiles(field):
    leading = field.shape[:-2]
    tiled = field.reshape(leading + (N_LAT, CLAT, N_LON, CLON))
    tiled = jnp.moveaxis(tiled, -3, -2)
    return tiled.reshape(leading + (N_LAT, N_LON, CLAT * CLON))


def from_tiles(field):
    leading = field.shape[:-3]
    tiled = field.reshape(leading + (N_LAT, N_LON, CLAT, CLON))
    tiled = jnp.moveaxis(tiled, -2, -3)
    return tiled.reshape(leading + (NLAT, NLON))


def regrid(source, index, weight):
    index_tiles = to_tiles(index)
    source_tiles = jnp.broadcast_to(to_tiles(source)[None], index_tiles.shape)
    picked = jnp.take_along_axis(source_tiles, index_tiles, axis=-1)
    return jnp.sum(weight * from_tiles(picked), axis=0)


def model_step(field, mixing, velocity, coupling, sea, partner, is_atmosphere):
    lat_padded = jnp.pad(field, ((0, 0), (2, 2), (0, 0)))
    lon_padded = jnp.concatenate([field[:, :, -2:], field, field[:, :, :2]], axis=2)
    moved = stencil(field, lat_padded, lon_padded, velocity[0], velocity[1])
    if is_atmosphere:
        forcing = coupling * sea * (partner - field[0])
    else:
        forcing = coupling * sea * partner
    moved = moved.at[0].add(forcing)
    solved = column_solve(moved, mixing)
    if is_atmosphere:
        return solved, forcing
    return solved, solved[0]


def reference(state, prev_surface, mixing, velocity, coupling, sea_mask, interp_index, interp_weight):
    sea = sea_mask.astype(jnp.float32)
    atmos = state[0]
    fluxes = []
    for step_index in range(NSTEP):
        partner = regrid(prev_surface[step_index], interp_index[0], interp_weight[0])
        atmos, flux_now = model_step(atmos, mixing[0], velocity[0], coupling[0], sea[0], partner, True)
        fluxes.append(flux_now)
    ocean = state[1]
    temps = []
    for step_index in range(NSTEP):
        partner = regrid(fluxes[step_index], interp_index[1], interp_weight[1])
        ocean, top_now = model_step(ocean, mixing[1], velocity[1], coupling[1], sea[1], partner, False)
        temps.append(top_now)
    return jnp.stack([atmos, ocean]), jnp.stack([jnp.stack(fluxes), jnp.stack(temps)])
```

```python
import functools

import jax
import jax.numpy as jnp
from jax import lax
from jax.experimental import pallas as pl
from jax.experimental.pallas import tpu as pltpu
from jax.sharding import PartitionSpec as P

SMOOTHING = 0.15
MESH = pl.DeviceIdType.MESH
PAD = 8
REACH = 2
SUB = 8


def lane_gather(values, lanes):
    return jnp.take_along_axis(values, lanes, axis=1, mode="promise_in_bounds")


def regrid(source, index, weight):
    points, rows, cols = index.shape
    shift = cols.bit_length() - 1
    parts = []
    for top in range(0, rows, SUB):
        where = [index[j, top : top + SUB, :] for j in range(points)]
        lanes = [lax.bitwise_and(w, cols - 1) for w in where]
        owners = [lax.shift_right_logical(w, shift) for w in where]
        picked = [jnp.zeros((SUB, cols), jnp.float32)] * points
        for row in range(rows):
            line = jnp.broadcast_to(source[row : row + 1, :], (SUB, cols))
            for j in range(points):
                picked[j] = jnp.where(owners[j] == row, lane_gather(line, lanes[j]), picked[j])
        total = weight[0, top : top + SUB, :] * picked[0]
        for j in range(1, points):
            total = total + weight[j, top : top + SUB, :] * picked[j]
        parts.append(total)
    return jnp.concatenate(parts, axis=0)


def kernel(
    sizes,
    state,
    prev,
    mixing,
    velocity,
    coupling,
    sea_mask,
    interp_index,
    interp_weight,
    new_state,
    series,
    ext,
    src,
    mix,
    vel,
    cpl,
    sea,
    idx,
    wgt,
    part,
    flux,
    y,
    lon_out,
    lon_in,
    in_sem,
    src_sem,
    lat_send,
    lat_recv,
    lon_send,
    lon_recv,
    flux_send,
    flux_recv,
):
    n_lat, n_lon, steps, levels, rows, cols = sizes
    comp, lat, lon = (lax.axis_index(a) for a in ("comp", "lat", "lon"))
    is_atmosphere = comp == 0
    is_ocean = comp != 0
    has_before = lat > 0
    has_after = lat < n_lat - 1
    before, after = {"lat": lat - 1}, {"lat": lat + 1}
    west, east = {"lon": lax.rem(lon + n_lon - 1, n_lon)}, {"lon": lax.rem(lon + 1, n_lon)}
    partner = {"comp": 1 - comp}
    own = pl.ds(PAD, rows)

    loads = [
        pltpu.make_async_copy(a, b, in_sem.at[i])
        for i, (a, b) in enumerate(
            (
                (state.at[0], ext.at[0, :, own, :]),
                (interp_index.at[0], idx),
                (interp_weight.at[0], wgt),
                (coupling.at[0], cpl),
                (sea_mask.at[0], sea),
                (velocity.at[0], vel),
                (mixing.at[0], mix),
            )
        )
    ]
    sources = [pltpu.make_async_copy(prev.at[s], src.at[s], src_sem.at[s]) for s in range(steps)]

    def remote(a, b, send, recv, device):
        return pltpu.make_async_remote_copy(
            src_ref=a, dst_ref=b, send_sem=send, recv_sem=recv, device_id=device, device_id_type=MESH
        )

    low, high = pl.ds(PAD, REACH), pl.ds(PAD + rows - REACH, REACH)
    halo_low, halo_high = pl.ds(PAD - REACH, REACH), pl.ds(PAD + rows, REACH)
    to_before, to_after, to_west, to_east, to_ocean = [], [], [], [], []
    for s in range(steps):
        to_before.append(
            remote(ext.at[s, :, low, :], ext.at[s, :, halo_high, :], lat_send.at[s, 0], lat_recv.at[s, 0], before)
        )
        to_after.append(
            remote(ext.at[s, :, high, :], ext.at[s, :, halo_low, :], lat_send.at[s, 1], lat_recv.at[s, 1], after)
        )
        to_west.append(remote(lon_out.at[s], lon_in.at[s, 0], lon_send.at[s, 0], lon_recv.at[s, 0], west))
        to_east.append(remote(lon_out.at[s], lon_in.at[s, 1], lon_send.at[s, 1], lon_recv.at[s, 1], east))
        to_ocean.append(remote(flux.at[s], src.at[s], flux_send.at[s], flux_recv.at[s], partner))

    barrier = pltpu.get_barrier_semaphore()

    @pl.when(has_before)
    def _():
        pl.semaphore_signal(barrier, inc=1, device_id=before, device_id_type=MESH)

    @pl.when(has_after)
    def _():
        pl.semaphore_signal(barrier, inc=1, device_id=after, device_id_type=MESH)

    for side in (west, east):
        pl.semaphore_signal(barrier, inc=1, device_id=side, device_id_type=MESH)

    @pl.when(is_ocean)
    def _():
        pl.semaphore_signal(barrier, inc=1, device_id=partner, device_id_type=MESH)

    @pl.when(is_atmosphere)
    def _():
        for copy in sources:
            copy.start()

    for copy in loads:
        copy.start()

    lane = lax.broadcasted_iota(jnp.int32, (rows, cols), 1)

    def pack(s):
        packed = jnp.zeros((rows, cols), jnp.float32)
        for level in range(levels):
            turned = pltpu.roll(ext[s, level, own, :], (4 * level + REACH) % cols, 1)
            packed = jnp.where((lane >= 4 * level) & (lane < 4 * level + 4), turned, packed)
        lon_out[s] = packed

    loads[0].wait()
    pack(0)
    nothing = jnp.zeros((steps, levels, REACH, cols), jnp.float32)

    @pl.when(jnp.logical_not(has_before))
    def _():
        ext[:, :, halo_low, :] = nothing

    @pl.when(jnp.logical_not(has_after))
    def _():
        ext[:, :, halo_high, :] = nothing

    for copy in loads[1:5]:
        copy.wait()
    rate = cpl[...] * sea[...].astype(jnp.float32)

    @pl.when(is_atmosphere)
    def _():
        sources[0].wait()
        part[0] = regrid(src.at[0], idx, wgt)
        flux[0] = rate * (part[0] - ext[0, 0, own, :])

    edges = has_before.astype(jnp.int32) + has_after.astype(jnp.int32)
    pl.semaphore_wait(barrier, 2 + edges + is_atmosphere.astype(jnp.int32))

    def send_halo(s):
        @pl.when(has_before)
        def _():
            to_before[s].start()

        @pl.when(has_after)
        def _():
            to_after[s].start()

        to_west[s].start()
        to_east[s].start()

    @pl.when(is_atmosphere)
    def _():
        to_ocean[0].start()

    send_halo(0)

    loads[5].wait()
    loads[6].wait()
    east_speed, north_speed = vel[0] * (1.0 / 12.0), vel[1] * (1.0 / 12.0)
    centre = 1.0 - 4.0 * SMOOTHING
    lon_m2, lon_m1 = -east_speed, SMOOTHING + 8.0 * east_speed
    lon_p1, lon_p2 = SMOOTHING - 8.0 * east_speed, east_speed
    lat_m2, lat_m1 = -north_speed, SMOOTHING + 8.0 * north_speed
    lat_p1, lat_p2 = SMOOTHING - 8.0 * north_speed, north_speed
    own_m2, own_m1 = jnp.where(lane < 2, 0.0, lon_m2), jnp.where(lane < 1, 0.0, lon_m1)
    own_p1 = jnp.where(lane >= cols - 1, 0.0, lon_p1)
    own_p2 = jnp.where(lane >= cols - 2, 0.0, lon_p2)
    place = lax.bitwise_and(lane, 3)
    rim = lax.bitwise_and(place + (cols - REACH), cols - 1)
    spread = lambda c, keep: jnp.where(keep, lane_gather(c, rim), 0.0)
    rim_p2 = spread(lon_p2, place < 2)
    rim_p1 = spread(lon_p1, place == 1)
    rim_m2 = spread(lon_m2, place >= 2)
    rim_m1 = spread(lon_m1, place == 2)
    on_rim = (lane < REACH) | (lane >= cols - REACH)

    inverse, ratio = [None] * levels, [None] * levels
    for level in range(levels - 1, -1, -1):
        pivot = 1.0
        if level < levels - 1:
            pivot = pivot + mix[level] * (1.0 - ratio[level + 1])
        if level > 0:
            pivot = pivot + mix[level - 1]
        inverse[level] = 1.0 / pivot
        if level > 0:
            ratio[level] = mix[level - 1] * inverse[level]

    def own_part(s):
        for level in range(levels):
            x = ext[s, level, own, :]
            y[level] = (
                centre * x
                + own_m2 * pltpu.roll(x, 2, 1)
                + own_m1 * pltpu.roll(x, 1, 1)
                + own_p1 * pltpu.roll(x, cols - 1, 1)
                + own_p2 * pltpu.roll(x, cols - 2, 1)
            )

    for s in range(steps):
        own_part(s)
        if s + 1 < steps:

            @pl.when(is_atmosphere)
            def _():
                sources[s + 1].wait()
                part[s + 1] = regrid(src.at[s + 1], idx, wgt)

        @pl.when(has_after)
        def _():
            to_before[s].wait_recv()

        @pl.when(has_before)
        def _():
            to_after[s].wait_recv()

        to_west[s].wait_recv()
        to_east[s].wait_recv()
        from_east, from_west = lon_in[s, 0], lon_in[s, 1]
        rims = (
            rim_p2 * pltpu.roll(from_east, cols - 2, 1)
            + rim_p1 * pltpu.roll(from_east, cols - 1, 1)
            + rim_m2 * pltpu.roll(from_west, 2, 1)
            + rim_m1 * pltpu.roll(from_west, 1, 1)
        )
        values = [None] * levels
        for level in range(levels - 1, -1, -1):
            total = (
                y[level]
                + lat_m2 * ext[s, level, pl.ds(PAD - 2, rows), :]
                + lat_m1 * ext[s, level, pl.ds(PAD - 1, rows), :]
                + lat_p1 * ext[s, level, pl.ds(PAD + 1, rows), :]
                + lat_p2 * ext[s, level, pl.ds(PAD + 2, rows), :]
                + jnp.where(on_rim, pltpu.roll(rims, (cols - REACH - 4 * level) % cols, 1), 0.0)
            )
            if level < levels - 1:
                total = total + mix[level] * values[level + 1]
            if level > 0:
                values[level] = total * inverse[level]
            else:
                y[0] = total

        @pl.when(is_ocean)
        def _():
            to_ocean[s].wait_recv()
            forcing = rate * regrid(src.at[s], idx, wgt)
            part[s] = forcing

        if s == 0:
            forcing = jnp.where(is_atmosphere, flux[0], part[0])
        else:
            forcing = jnp.where(is_atmosphere, flux[s], part[s])
        x = (y[0] + forcing) * inverse[0]
        series[0, s] = jnp.where(is_atmosphere, forcing, x)
        last = s + 1 == steps
        if not last:

            @pl.when(is_atmosphere)
            def _():
                flux[s + 1] = rate * (part[s + 1] - x)
                to_ocean[s + 1].start()

        for level in range(levels):
            if level > 0:
                x = values[level] + ratio[level] * x
            if last:
                new_state[0, level] = x
            else:
                ext[s + 1, level, own, :] = x
        if not last:
            pack(s + 1)
            send_halo(s + 1)

    for s in range(steps):

        @pl.when(is_atmosphere)
        def _():
            to_ocean[s].wait_send()

        @pl.when(has_before)
        def _():
            to_before[s].wait_send()

        @pl.when(has_after)
        def _():
            to_after[s].wait_send()

        to_west[s].wait_send()
        to_east[s].wait_send()


def per_device(n_lat, n_lon, state, prev, mixing, velocity, coupling, sea_mask, index, weight):
    levels, rows, cols = state.shape[1:]
    steps, points = prev.shape[0], index.shape[1]
    tile = (rows, cols)
    floats = lambda *lead: pltpu.VMEM(lead + tile, jnp.float32)
    dma = pltpu.SemaphoreType.DMA
    return pl.pallas_call(
        functools.partial(kernel, (n_lat, n_lon, steps, levels, rows, cols)),
        out_shape=(
            jax.ShapeDtypeStruct(state.shape, jnp.float32),
            jax.ShapeDtypeStruct((1, steps) + tile, jnp.float32),
        ),
        in_specs=[pl.BlockSpec(memory_space=pltpu.HBM)] * 8,
        out_specs=[pl.BlockSpec(memory_space=pltpu.VMEM)] * 2,
        scratch_shapes=[
            pltpu.VMEM((steps, levels, rows + 2 * PAD, cols), jnp.float32),
            floats(steps),
            floats(levels - 1),
            floats(2),
            floats(),
            pltpu.VMEM(tile, jnp.int32),
            pltpu.VMEM((points,) + tile, jnp.int32),
            floats(points),
            floats(steps),
            floats(steps),
            floats(levels),
            floats(steps),
            floats(steps, 2),
            dma((7,)),
            dma((steps,)),
            dma((steps, 2)),
            dma((steps, 2)),
            dma((steps, 2)),
            dma((steps, 2)),
            dma((steps,)),
            dma((steps,)),
        ],
        compiler_params=pltpu.CompilerParams(collective_id=0, has_side_effects=True),
        name="coupled_window",
    )(state, prev, mixing, velocity, coupling, sea_mask, index, weight)


def solution(mesh):
    in_specs = (
        P("comp", None, "lat", "lon"),
        P(None, "lat", "lon"),
        P("comp", None, "lat", "lon"),
        P("comp", None, "lat", "lon"),
        P("comp", "lat", "lon"),
        P("comp", "lat", "lon"),
        P("comp", None, "lat", "lon"),
        P("comp", None, "lat", "lon"),
    )
    out_specs = (P("comp", None, "lat", "lon"), P("comp", None, "lat", "lon"))
    return jax.shard_map(
        functools.partial(per_device, mesh.shape["lat"], mesh.shape["lon"]),
        mesh=mesh,
        in_specs=in_specs,
        out_specs=out_specs,
        check_vma=False,
    )
```

```python
import functools

import jax
import jax.numpy as jnp
from jax import lax
from jax.experimental import pallas as pl
from jax.experimental.pallas import tpu as pltpu
from jax.sharding import PartitionSpec as P

SMOOTHING = 0.15
MESH = pl.DeviceIdType.MESH
PAD = 8
REACH = 2
SUB = 8


def lane_gather(values, lanes):
    return jnp.take_along_axis(values, lanes, axis=1, mode="promise_in_bounds")


def regrid(source, index, weight):
    points, rows, cols = index.shape
    shift = cols.bit_length() - 1
    parts = []
    for top in range(0, rows, SUB):
        where = [index[j, top : top + SUB, :] for j in range(points)]
        lanes = [lax.bitwise_and(w, cols - 1) for w in where]
        owners = [lax.shift_right_logical(w, shift) for w in where]
        picked = [jnp.zeros((SUB, cols), jnp.float32)] * points
        for row in range(rows):
            line = jnp.broadcast_to(source[row : row + 1, :], (SUB, cols))
            for j in range(points):
                picked[j] = jnp.where(owners[j] == row, lane_gather(line, lanes[j]), picked[j])
        total = weight[0, top : top + SUB, :] * picked[0]
        for j in range(1, points):
            total = total + weight[j, top : top + SUB, :] * picked[j]
        parts.append(total)
    return jnp.concatenate(parts, axis=0)


def kernel(
    sizes,
    state,
    prev,
    mixing,
    velocity,
    coupling,
    sea_mask,
    interp_index,
    interp_weight,
    new_state,
    series,
    ext,
    src,
    mix,
    vel,
    cpl,
    sea,
    idx,
    wgt,
    part,
    flux,
    y,
    lon_out,
    lon_in,
    in_sem,
    src_sem,
    lat_send,
    lat_recv,
    lon_send,
    lon_recv,
    flux_send,
    flux_recv,
    result,
    top,
    out_sem,
    top_sem,
):
    n_lat, n_lon, steps, levels, rows, cols = sizes
    comp, lat, lon = (lax.axis_index(a) for a in ("comp", "lat", "lon"))
    is_atmosphere = comp == 0
    is_ocean = comp != 0
    has_before = lat > 0
    has_after = lat < n_lat - 1
    before, after = {"lat": lat - 1}, {"lat": lat + 1}
    west, east = {"lon": lax.rem(lon + n_lon - 1, n_lon)}, {"lon": lax.rem(lon + 1, n_lon)}
    partner = {"comp": 1 - comp}
    own = pl.ds(PAD, rows)

    loads = [
        pltpu.make_async_copy(a, b, in_sem.at[i])
        for i, (a, b) in enumerate(
            (
                (state.at[0], ext.at[0, :, own, :]),
                (interp_index.at[0], idx),
                (interp_weight.at[0], wgt),
                (coupling.at[0], cpl),
                (sea_mask.at[0], sea),
                (velocity.at[0], vel),
                (mixing.at[0], mix),
            )
        )
    ]
    sources = [pltpu.make_async_copy(prev.at[s], src.at[s], src_sem.at[s]) for s in range(steps)]

    def remote(a, b, send, recv, device):
        return pltpu.make_async_remote_copy(
            src_ref=a, dst_ref=b, send_sem=send, recv_sem=recv, device_id=device, device_id_type=MESH
        )

    low, high = pl.ds(PAD, REACH), pl.ds(PAD + rows - REACH, REACH)
    halo_low, halo_high = pl.ds(PAD - REACH, REACH), pl.ds(PAD + rows, REACH)
    to_before, to_after, to_west, to_east, to_ocean = [], [], [], [], []
    for s in range(steps):
        to_before.append(
            remote(ext.at[s, :, low, :], ext.at[s, :, halo_high, :], lat_send.at[s, 0], lat_recv.at[s, 0], before)
        )
        to_after.append(
            remote(ext.at[s, :, high, :], ext.at[s, :, halo_low, :], lat_send.at[s, 1], lat_recv.at[s, 1], after)
        )
        to_west.append(remote(lon_out.at[s], lon_in.at[s, 0], lon_send.at[s, 0], lon_recv.at[s, 0], west))
        to_east.append(remote(lon_out.at[s], lon_in.at[s, 1], lon_send.at[s, 1], lon_recv.at[s, 1], east))
        to_ocean.append(remote(flux.at[s], src.at[s], flux_send.at[s], flux_recv.at[s], partner))

    results = [pltpu.make_async_copy(result.at[i], new_state.at[0, i], out_sem.at[i]) for i in range(levels)]
    tops = [pltpu.make_async_copy(top.at[s], series.at[0, s], top_sem.at[s]) for s in range(steps)]

    barrier = pltpu.get_barrier_semaphore()

    @pl.when(has_before)
    def _():
        pl.semaphore_signal(barrier, inc=1, device_id=before, device_id_type=MESH)

    @pl.when(has_after)
    def _():
        pl.semaphore_signal(barrier, inc=1, device_id=after, device_id_type=MESH)

    for side in (west, east):
        pl.semaphore_signal(barrier, inc=1, device_id=side, device_id_type=MESH)

    @pl.when(is_ocean)
    def _():
        pl.semaphore_signal(barrier, inc=1, device_id=partner, device_id_type=MESH)

    @pl.when(is_atmosphere)
    def _():
        for copy in sources:
            copy.start()

    for copy in loads:
        copy.start()

    lane = lax.broadcasted_iota(jnp.int32, (rows, cols), 1)

    def pack(s):
        packed = jnp.zeros((rows, cols), jnp.float32)
        for level in range(levels):
            turned = pltpu.roll(ext[s, level, own, :], (4 * level + REACH) % cols, 1)
            packed = jnp.where((lane >= 4 * level) & (lane < 4 * level + 4), turned, packed)
        lon_out[s] = packed

    loads[0].wait()
    pack(0)
    nothing = jnp.zeros((steps, levels, REACH, cols), jnp.float32)

    @pl.when(jnp.logical_not(has_before))
    def _():
        ext[:, :, halo_low, :] = nothing

    @pl.when(jnp.logical_not(has_after))
    def _():
        ext[:, :, halo_high, :] = nothing

    edges = has_before.astype(jnp.int32) + has_after.astype(jnp.int32)
    pl.semaphore_wait(barrier, 2 + edges + is_atmosphere.astype(jnp.int32))

    def send_halo(s):
        @pl.when(has_before)
        def _():
            to_before[s].start()

        @pl.when(has_after)
        def _():
            to_after[s].start()

        to_west[s].start()
        to_east[s].start()

    send_halo(0)
    for copy in loads[1:5]:
        copy.wait()
    rate = cpl[...] * sea[...].astype(jnp.float32)

    @pl.when(is_atmosphere)
    def _():
        sources[0].wait()
        flux[0] = rate * (regrid(src.at[0], idx, wgt) - ext[0, 0, own, :])
        to_ocean[0].start()

    loads[5].wait()
    loads[6].wait()
    east_speed, north_speed = vel[0] * (1.0 / 12.0), vel[1] * (1.0 / 12.0)
    centre = 1.0 - 4.0 * SMOOTHING
    lon_m2, lon_m1 = -east_speed, SMOOTHING + 8.0 * east_speed
    lon_p1, lon_p2 = SMOOTHING - 8.0 * east_speed, east_speed
    lat_m2, lat_m1 = -north_speed, SMOOTHING + 8.0 * north_speed
    lat_p1, lat_p2 = SMOOTHING - 8.0 * north_speed, north_speed
    own_m2, own_m1 = jnp.where(lane < 2, 0.0, lon_m2), jnp.where(lane < 1, 0.0, lon_m1)
    own_p1 = jnp.where(lane >= cols - 1, 0.0, lon_p1)
    own_p2 = jnp.where(lane >= cols - 2, 0.0, lon_p2)
    place = lax.bitwise_and(lane, 3)
    rim = lax.bitwise_and(place + (cols - REACH), cols - 1)
    spread = lambda c, keep: jnp.where(keep, lane_gather(c, rim), 0.0)
    rim_p2 = spread(lon_p2, place < 2)
    rim_p1 = spread(lon_p1, place == 1)
    rim_m2 = spread(lon_m2, place >= 2)
    rim_m1 = spread(lon_m1, place == 2)
    on_rim = (lane < REACH) | (lane >= cols - REACH)

    inverse, ratio = [None] * levels, [None] * levels
    for level in range(levels - 1, -1, -1):
        pivot = 1.0
        if level < levels - 1:
            pivot = pivot + mix[level] * (1.0 - ratio[level + 1])
        if level > 0:
            pivot = pivot + mix[level - 1]
        inverse[level] = 1.0 / pivot
        if level > 0:
            ratio[level] = mix[level - 1] * inverse[level]

    def own_part(s):
        for level in range(levels):
            x = ext[s, level, own, :]
            y[level] = (
                centre * x
                + own_m2 * pltpu.roll(x, 2, 1)
                + own_m1 * pltpu.roll(x, 1, 1)
                + own_p1 * pltpu.roll(x, cols - 1, 1)
                + own_p2 * pltpu.roll(x, cols - 2, 1)
            )

    for s in range(steps):
        own_part(s)
        if s + 1 < steps:

            @pl.when(is_atmosphere)
            def _():
                sources[s + 1].wait()
                part[s + 1] = regrid(src.at[s + 1], idx, wgt)

        @pl.when(has_after)
        def _():
            to_before[s].wait_recv()

        @pl.when(has_before)
        def _():
            to_after[s].wait_recv()

        to_west[s].wait_recv()
        to_east[s].wait_recv()
        from_east, from_west = lon_in[s, 0], lon_in[s, 1]
        rims = (
            rim_p2 * pltpu.roll(from_east, cols - 2, 1)
            + rim_p1 * pltpu.roll(from_east, cols - 1, 1)
            + rim_m2 * pltpu.roll(from_west, 2, 1)
            + rim_m1 * pltpu.roll(from_west, 1, 1)
        )
        values = [None] * levels
        for level in range(levels - 1, -1, -1):
            total = (
                y[level]
                + lat_m2 * ext[s, level, pl.ds(PAD - 2, rows), :]
                + lat_m1 * ext[s, level, pl.ds(PAD - 1, rows), :]
                + lat_p1 * ext[s, level, pl.ds(PAD + 1, rows), :]
                + lat_p2 * ext[s, level, pl.ds(PAD + 2, rows), :]
                + jnp.where(on_rim, pltpu.roll(rims, (cols - REACH - 4 * level) % cols, 1), 0.0)
            )
            if level < levels - 1:
                total = total + mix[level] * values[level + 1]
            if level > 0:
                values[level] = total * inverse[level]
            else:
                y[0] = total

        @pl.when(is_ocean)
        def _():
            to_ocean[s].wait_recv()
            forcing = rate * regrid(src.at[s], idx, wgt)
            part[s] = forcing

        forcing = jnp.where(is_atmosphere, flux[s], part[s])
        x = (y[0] + forcing) * inverse[0]
        top[s] = jnp.where(is_atmosphere, forcing, x)
        tops[s].start()
        last = s + 1 == steps
        if not last:

            @pl.when(is_atmosphere)
            def _():
                flux[s + 1] = rate * (part[s + 1] - x)
                to_ocean[s + 1].start()

        for level in range(levels):
            if level > 0:
                x = values[level] + ratio[level] * x
            if last:
                result[level] = x
                results[level].start()
            else:
                ext[s + 1, level, own, :] = x
        if not last:
            pack(s + 1)
            send_halo(s + 1)

    for s in range(steps):

        @pl.when(is_atmosphere)
        def _():
            to_ocean[s].wait_send()

        @pl.when(has_before)
        def _():
            to_before[s].wait_send()

        @pl.when(has_after)
        def _():
            to_after[s].wait_send()

        to_west[s].wait_send()
        to_east[s].wait_send()

    for copy in tops + results:
        copy.wait()


def hand_over(state_in, series_in, state_out, series_out, sem):
    copies = [
        pltpu.make_async_copy(series_in, series_out, sem.at[0]),
        pltpu.make_async_copy(state_in, state_out, sem.at[1]),
    ]
    for copy in copies:
        copy.start()
    for copy in copies:
        copy.wait()


def per_device(n_lat, n_lon, state, prev, mixing, velocity, coupling, sea_mask, index, weight):
    levels, rows, cols = state.shape[1:]
    steps, points = prev.shape[0], index.shape[1]
    tile = (rows, cols)
    floats = lambda *lead: pltpu.VMEM(lead + tile, jnp.float32)
    dma = pltpu.SemaphoreType.DMA
    shapes = (
        jax.ShapeDtypeStruct(state.shape, jnp.float32),
        jax.ShapeDtypeStruct((1, steps) + tile, jnp.float32),
    )
    outs = pl.pallas_call(
        functools.partial(kernel, (n_lat, n_lon, steps, levels, rows, cols)),
        out_shape=shapes,
        in_specs=[pl.BlockSpec(memory_space=pl.ANY)] * 8,
        out_specs=[pl.BlockSpec(memory_space=pl.ANY)] * 2,
        scratch_shapes=[
            pltpu.VMEM((steps, levels, rows + 2 * PAD, cols), jnp.float32),
            floats(steps),
            floats(levels - 1),
            floats(2),
            floats(),
            pltpu.VMEM(tile, jnp.int32),
            pltpu.VMEM((points,) + tile, jnp.int32),
            floats(points),
            floats(steps),
            floats(steps),
            floats(levels),
            floats(steps),
            floats(steps, 2),
            dma((7,)),
            dma((steps,)),
            dma((steps, 2)),
            dma((steps, 2)),
            dma((steps, 2)),
            dma((steps, 2)),
            dma((steps,)),
            dma((steps,)),
            floats(levels),
            floats(steps),
            dma((levels,)),
            dma((steps,)),
        ],
        compiler_params=pltpu.CompilerParams(collective_id=0, has_side_effects=True),
        name="coupled_window",
    )(state, prev, mixing, velocity, coupling, sea_mask, index, weight)
    return pl.pallas_call(
        hand_over,
        out_shape=shapes,
        in_specs=[pl.BlockSpec(memory_space=pl.ANY)] * 2,
        out_specs=[pl.BlockSpec(memory_space=pl.ANY)] * 2,
        scratch_shapes=[dma((2,))],
        name="hand_over",
    )(*outs)


def solution(mesh):
    in_specs = (
        P("comp", None, "lat", "lon"),
        P(None, "lat", "lon"),
        P("comp", None, "lat", "lon"),
        P("comp", None, "lat", "lon"),
        P("comp", "lat", "lon"),
        P("comp", "lat", "lon"),
        P("comp", None, "lat", "lon"),
        P("comp", None, "lat", "lon"),
    )
    out_specs = (P("comp", None, "lat", "lon"), P("comp", None, "lat", "lon"))
    return jax.shard_map(
        functools.partial(per_device, mesh.shape["lat"], mesh.shape["lon"]),
        mesh=mesh,
        in_specs=in_specs,
        out_specs=out_specs,
        check_vma=False,
    )
```

```python
import functools

import jax
import jax.numpy as jnp
from jax import lax
from jax.experimental import pallas as pl
from jax.experimental.pallas import tpu as pltpu
from jax.sharding import PartitionSpec as P

SMOOTHING = 0.15
MESH = pl.DeviceIdType.MESH
PAD = 8
REACH = 2
VMEM_BYTES = 8 * 2**20
GROUPS = 4
SUB = 8


def lane_gather(values, lanes):
    return jnp.take_along_axis(values, lanes, axis=1, mode="promise_in_bounds")


def regrid(source, index, weight):
    points, rows, cols = index.shape
    shift = cols.bit_length() - 1
    parts = []
    for top in range(0, rows, SUB):
        where = [index[j, top : top + SUB, :] for j in range(points)]
        lanes = [lax.bitwise_and(w, cols - 1) for w in where]
        owners = [lax.shift_right_logical(w, shift) for w in where]
        picked = [jnp.zeros((SUB, cols), jnp.float32)] * points
        for row in range(rows):
            line = jnp.broadcast_to(source[row : row + 1, :], (SUB, cols))
            for j in range(points):
                picked[j] = jnp.where(owners[j] == row, lane_gather(line, lanes[j]), picked[j])
        total = weight[0, top : top + SUB, :] * picked[0]
        for j in range(1, points):
            total = total + weight[j, top : top + SUB, :] * picked[j]
        parts.append(total)
    return jnp.concatenate(parts, axis=0)


def kernel(
    sizes,
    state,
    prev,
    mixing,
    velocity,
    coupling,
    sea_mask,
    interp_index,
    interp_weight,
    new_state,
    series,
    ext,
    src,
    mix,
    vel,
    cpl,
    sea,
    idx,
    wgt,
    part,
    flux,
    y,
    lon_out,
    lon_in,
    in_sem,
    src_sem,
    lat_send,
    lat_recv,
    lon_send,
    lon_recv,
    flux_send,
    flux_recv,
):
    n_lat, n_lon, steps, levels, rows, cols = sizes
    comp, lat, lon = (lax.axis_index(a) for a in ("comp", "lat", "lon"))
    is_atmosphere = comp == 0
    is_ocean = comp != 0
    has_before = lat > 0
    has_after = lat < n_lat - 1
    before, after = {"lat": lat - 1}, {"lat": lat + 1}
    west, east = {"lon": lax.rem(lon + n_lon - 1, n_lon)}, {"lon": lax.rem(lon + 1, n_lon)}
    partner = {"comp": 1 - comp}
    own = pl.ds(PAD, rows)

    loads = [
        pltpu.make_async_copy(a, b, in_sem.at[i])
        for i, (a, b) in enumerate(
            (
                (state.at[0], ext.at[0, :, own, :]),
                (interp_index.at[0], idx),
                (interp_weight.at[0], wgt),
                (coupling.at[0], cpl),
                (sea_mask.at[0], sea),
                (velocity.at[0], vel),
                (mixing.at[0], mix),
            )
        )
    ]
    sources = [pltpu.make_async_copy(prev.at[s], src.at[s], src_sem.at[s]) for s in range(steps)]

    def remote(a, b, send, recv, device):
        return pltpu.make_async_remote_copy(
            src_ref=a, dst_ref=b, send_sem=send, recv_sem=recv, device_id=device, device_id_type=MESH
        )

    low, high = pl.ds(PAD, REACH), pl.ds(PAD + rows - REACH, REACH)
    halo_low, halo_high = pl.ds(PAD - REACH, REACH), pl.ds(PAD + rows, REACH)
    to_before, to_after, to_west, to_east, to_ocean = [], [], [], [], []
    for s in range(steps):
        to_before.append(
            remote(ext.at[s, :, low, :], ext.at[s, :, halo_high, :], lat_send.at[s, 0], lat_recv.at[s, 0], before)
        )
        to_after.append(
            remote(ext.at[s, :, high, :], ext.at[s, :, halo_low, :], lat_send.at[s, 1], lat_recv.at[s, 1], after)
        )
        to_west.append(remote(lon_out.at[s], lon_in.at[s, 0], lon_send.at[s, 0], lon_recv.at[s, 0], west))
        to_east.append(remote(lon_out.at[s], lon_in.at[s, 1], lon_send.at[s, 1], lon_recv.at[s, 1], east))
        to_ocean.append(remote(flux.at[s], src.at[s], flux_send.at[s], flux_recv.at[s], partner))

    barrier = pltpu.get_barrier_semaphore()

    @pl.when(has_before)
    def _():
        pl.semaphore_signal(barrier, inc=1, device_id=before, device_id_type=MESH)

    @pl.when(has_after)
    def _():
        pl.semaphore_signal(barrier, inc=1, device_id=after, device_id_type=MESH)

    for side in (west, east):
        pl.semaphore_signal(barrier, inc=1, device_id=side, device_id_type=MESH)

    @pl.when(is_ocean)
    def _():
        pl.semaphore_signal(barrier, inc=1, device_id=partner, device_id_type=MESH)

    @pl.when(is_atmosphere)
    def _():
        for copy in sources:
            copy.start()

    for copy in loads:
        copy.start()

    lane = lax.broadcasted_iota(jnp.int32, (rows, cols), 1)

    def pack(s):
        packed = jnp.zeros((rows, cols), jnp.float32)
        for level in range(levels):
            turned = pltpu.roll(ext[s, level, own, :], (4 * level + REACH) % cols, 1)
            packed = jnp.where((lane >= 4 * level) & (lane < 4 * level + 4), turned, packed)
        lon_out[s] = packed

    loads[0].wait()
    pack(0)
    nothing = jnp.zeros((steps, levels, REACH, cols), jnp.float32)

    @pl.when(jnp.logical_not(has_before))
    def _():
        ext[:, :, halo_low, :] = nothing

    @pl.when(jnp.logical_not(has_after))
    def _():
        ext[:, :, halo_high, :] = nothing

    edges = has_before.astype(jnp.int32) + has_after.astype(jnp.int32)
    pl.semaphore_wait(barrier, 2 + edges + is_atmosphere.astype(jnp.int32))

    def send_halo(s):
        @pl.when(has_before)
        def _():
            to_before[s].start()

        @pl.when(has_after)
        def _():
            to_after[s].start()

        to_west[s].start()
        to_east[s].start()

    send_halo(0)
    for copy in loads[1:5]:
        copy.wait()
    rate = cpl[...] * sea[...].astype(jnp.float32)

    @pl.when(is_atmosphere)
    def _():
        sources[0].wait()
        flux[0] = rate * (regrid(src.at[0], idx, wgt) - ext[0, 0, own, :])
        to_ocean[0].start()

    loads[5].wait()
    loads[6].wait()
    east_speed, north_speed = vel[0] * (1.0 / 12.0), vel[1] * (1.0 / 12.0)
    centre = 1.0 - 4.0 * SMOOTHING
    lon_m2, lon_m1 = -east_speed, SMOOTHING + 8.0 * east_speed
    lon_p1, lon_p2 = SMOOTHING - 8.0 * east_speed, east_speed
    lat_m2, lat_m1 = -north_speed, SMOOTHING + 8.0 * north_speed
    lat_p1, lat_p2 = SMOOTHING - 8.0 * north_speed, north_speed
    own_m2, own_m1 = jnp.where(lane < 2, 0.0, lon_m2), jnp.where(lane < 1, 0.0, lon_m1)
    own_p1 = jnp.where(lane >= cols - 1, 0.0, lon_p1)
    own_p2 = jnp.where(lane >= cols - 2, 0.0, lon_p2)
    place = lax.bitwise_and(lane, 3)
    rim = lax.bitwise_and(place + (cols - REACH), cols - 1)
    spread = lambda c, keep: jnp.where(keep, lane_gather(c, rim), 0.0)
    rim_p2 = spread(lon_p2, place < 2)
    rim_p1 = spread(lon_p1, place == 1)
    rim_m2 = spread(lon_m2, place >= 2)
    rim_m1 = spread(lon_m1, place == 2)
    on_rim = (lane < REACH) | (lane >= cols - REACH)

    inverse, ratio = [None] * levels, [None] * levels
    for level in range(levels - 1, -1, -1):
        pivot = 1.0
        if level < levels - 1:
            pivot = pivot + mix[level] * (1.0 - ratio[level + 1])
        if level > 0:
            pivot = pivot + mix[level - 1]
        inverse[level] = 1.0 / pivot
        if level > 0:
            ratio[level] = mix[level - 1] * inverse[level]

    def own_part(s):
        for level in range(levels):
            x = ext[s, level, own, :]
            y[level] = (
                centre * x
                + own_m2 * pltpu.roll(x, 2, 1)
                + own_m1 * pltpu.roll(x, 1, 1)
                + own_p1 * pltpu.roll(x, cols - 1, 1)
                + own_p2 * pltpu.roll(x, cols - 2, 1)
            )

    for s in range(steps):
        own_part(s)
        if s + 1 < steps:

            @pl.when(is_atmosphere)
            def _():
                sources[s + 1].wait()
                part[s + 1] = regrid(src.at[s + 1], idx, wgt)

        @pl.when(has_after)
        def _():
            to_before[s].wait_recv()

        @pl.when(has_before)
        def _():
            to_after[s].wait_recv()

        to_west[s].wait_recv()
        to_east[s].wait_recv()
        from_east, from_west = lon_in[s, 0], lon_in[s, 1]
        rims = (
            rim_p2 * pltpu.roll(from_east, cols - 2, 1)
            + rim_p1 * pltpu.roll(from_east, cols - 1, 1)
            + rim_m2 * pltpu.roll(from_west, 2, 1)
            + rim_m1 * pltpu.roll(from_west, 1, 1)
        )
        values = [None] * levels
        for level in range(levels - 1, -1, -1):
            total = (
                y[level]
                + lat_m2 * ext[s, level, pl.ds(PAD - 2, rows), :]
                + lat_m1 * ext[s, level, pl.ds(PAD - 1, rows), :]
                + lat_p1 * ext[s, level, pl.ds(PAD + 1, rows), :]
                + lat_p2 * ext[s, level, pl.ds(PAD + 2, rows), :]
                + jnp.where(on_rim, pltpu.roll(rims, (cols - REACH - 4 * level) % cols, 1), 0.0)
            )
            if level < levels - 1:
                total = total + mix[level] * values[level + 1]
            if level > 0:
                values[level] = total * inverse[level]
            else:
                y[0] = total

        @pl.when(is_ocean)
        def _():
            to_ocean[s].wait_recv()
            forcing = rate * regrid(src.at[s], idx, wgt)
            part[s] = forcing

        forcing = jnp.where(is_atmosphere, flux[s], part[s])
        x = (y[0] + forcing) * inverse[0]
        series[0, s] = jnp.where(is_atmosphere, forcing, x)
        last = s + 1 == steps
        if not last:

            @pl.when(is_atmosphere)
            def _():
                flux[s + 1] = rate * (part[s + 1] - x)
                to_ocean[s + 1].start()

        for level in range(levels):
            if level > 0:
                x = values[level] + ratio[level] * x
            if last:
                new_state[0, level] = x
            else:
                ext[s + 1, level, own, :] = x
        if not last:
            pack(s + 1)
            send_halo(s + 1)

    for s in range(steps):

        @pl.when(is_atmosphere)
        def _():
            to_ocean[s].wait_send()

        @pl.when(has_before)
        def _():
            to_before[s].wait_send()

        @pl.when(has_after)
        def _():
            to_after[s].wait_send()

        to_west[s].wait_send()
        to_east[s].wait_send()


def hand_over(state_in, series_in, state_out, series_out, sem):
    levels = state_in.shape[1]
    group = pl.cdiv(levels, GROUPS)
    copies = [pltpu.make_async_copy(series_in, series_out, sem.at[GROUPS])]
    for i, first in enumerate(range(0, levels, group)):
        some = pl.ds(first, min(group, levels - first))
        copies.append(pltpu.make_async_copy(state_in.at[0, some], state_out.at[0, some], sem.at[i]))
    for copy in copies:
        copy.start()
    for copy in copies:
        copy.wait()


def per_device(n_lat, n_lon, state, prev, mixing, velocity, coupling, sea_mask, index, weight):
    levels, rows, cols = state.shape[1:]
    steps, points = prev.shape[0], index.shape[1]
    tile = (rows, cols)
    floats = lambda *lead: pltpu.VMEM(lead + tile, jnp.float32)
    dma = pltpu.SemaphoreType.DMA
    shapes = (
        jax.ShapeDtypeStruct(state.shape, jnp.float32),
        jax.ShapeDtypeStruct((1, steps) + tile, jnp.float32),
    )
    outs = pl.pallas_call(
        functools.partial(kernel, (n_lat, n_lon, steps, levels, rows, cols)),
        out_shape=tuple(pltpu.VMEM(s.shape, s.dtype) for s in shapes),
        in_specs=[pl.BlockSpec(memory_space=pltpu.HBM)] * 8,
        out_specs=[pl.BlockSpec(memory_space=pltpu.VMEM)] * 2,
        scratch_shapes=[
            pltpu.VMEM((steps, levels, rows + 2 * PAD, cols), jnp.float32),
            floats(steps),
            floats(levels - 1),
            floats(2),
            floats(),
            pltpu.VMEM(tile, jnp.int32),
            pltpu.VMEM((points,) + tile, jnp.int32),
            floats(points),
            floats(steps),
            floats(steps),
            floats(levels),
            floats(steps),
            floats(steps, 2),
            dma((7,)),
            dma((steps,)),
            dma((steps, 2)),
            dma((steps, 2)),
            dma((steps, 2)),
            dma((steps, 2)),
            dma((steps,)),
            dma((steps,)),
        ],
        compiler_params=pltpu.CompilerParams(collective_id=0, has_side_effects=True, vmem_limit_bytes=VMEM_BYTES),
        name="coupled_window",
    )(*(pltpu.with_memory_space_constraint(a, pltpu.HBM) for a in (state, prev, mixing, velocity, coupling, sea_mask, index, weight)))
    return pl.pallas_call(
        hand_over,
        out_shape=shapes,
        in_specs=[pl.BlockSpec(memory_space=pltpu.VMEM)] * 2,
        out_specs=[pl.BlockSpec(memory_space=pl.ANY)] * 2,
        scratch_shapes=[dma((GROUPS + 1,))],
        compiler_params=pltpu.CompilerParams(vmem_limit_bytes=VMEM_BYTES),
        name="hand_over",
    )(*outs)


def solution(mesh):
    in_specs = (
        P("comp", None, "lat", "lon"),
        P(None, "lat", "lon"),
        P("comp", None, "lat", "lon"),
        P("comp", None, "lat", "lon"),
        P("comp", "lat", "lon"),
        P("comp", "lat", "lon"),
        P("comp", None, "lat", "lon"),
        P("comp", None, "lat", "lon"),
    )
    out_specs = (P("comp", None, "lat", "lon"), P("comp", None, "lat", "lon"))
    return jax.shard_map(
        functools.partial(per_device, mesh.shape["lat"], mesh.shape["lon"]),
        mesh=mesh,
        in_specs=in_specs,
        out_specs=out_specs,
        check_vma=False,
    )
```

```python
import functools

import jax
import jax.numpy as jnp
from jax import lax
from jax.experimental import pallas as pl
from jax.experimental.pallas import tpu as pltpu
from jax.sharding import PartitionSpec as P

SMOOTHING = 0.15
MESH = pl.DeviceIdType.MESH
PAD = 8
REACH = 2
VMEM_BYTES = 8 * 2**20
GROUPS = 4
SUB = 8


def lane_gather(values, lanes):
    return jnp.take_along_axis(values, lanes, axis=1, mode="promise_in_bounds")


def regrid(source, index, weight):
    points, rows, cols = index.shape
    shift = cols.bit_length() - 1
    parts = []
    for top in range(0, rows, SUB):
        total = jnp.zeros((SUB, cols), jnp.float32)
        for j in range(points):
            where = index[j, top : top + SUB, :]
            lanes, owner = lax.bitwise_and(where, cols - 1), lax.shift_right_logical(where, shift)
            picked = jnp.zeros((SUB, cols), jnp.float32)
            for row in range(rows):
                line = jnp.broadcast_to(source[row : row + 1, :], (SUB, cols))
                picked = jnp.where(owner == row, lane_gather(line, lanes), picked)
            total = total + weight[j, top : top + SUB, :] * picked
        parts.append(total)
    return jnp.concatenate(parts, axis=0)


def kernel(
    sizes,
    state,
    prev,
    mixing,
    velocity,
    coupling,
    sea_mask,
    interp_index,
    interp_weight,
    new_state,
    series,
    ext,
    src,
    mix,
    vel,
    cpl,
    sea,
    idx,
    wgt,
    part,
    flux,
    y,
    lon_out,
    lon_in,
    in_sem,
    src_sem,
    lat_send,
    lat_recv,
    lon_send,
    lon_recv,
    flux_send,
    flux_recv,
):
    n_lat, n_lon, steps, levels, rows, cols = sizes
    comp, lat, lon = (lax.axis_index(a) for a in ("comp", "lat", "lon"))
    is_atmosphere = comp == 0
    is_ocean = comp != 0
    has_before = lat > 0
    has_after = lat < n_lat - 1
    before, after = {"lat": lat - 1}, {"lat": lat + 1}
    west, east = {"lon": lax.rem(lon + n_lon - 1, n_lon)}, {"lon": lax.rem(lon + 1, n_lon)}
    partner = {"comp": 1 - comp}
    own = pl.ds(PAD, rows)

    def chunks(count):
        size = pl.cdiv(count, GROUPS)
        return [pl.ds(first, min(size, count - first)) for first in range(0, count, size)]

    count = iter(range(3 * GROUPS + 1))
    load = lambda a, b: pltpu.make_async_copy(a, b, in_sem.at[next(count)])
    load_state = [load(state.at[0, c], ext.at[0, c, own, :]) for c in chunks(levels)]
    load_regrid = [
        load(a.at[0], b) for a, b in ((interp_index, idx), (interp_weight, wgt), (coupling, cpl), (sea_mask, sea))
    ]
    load_rest = [load(velocity.at[0], vel)]
    load_rest += [load(mixing.at[0, c], mix.at[c]) for c in chunks(levels - 1)]
    sources = [pltpu.make_async_copy(prev.at[s], src.at[s], src_sem.at[s]) for s in range(steps)]

    def remote(a, b, send, recv, device):
        return pltpu.make_async_remote_copy(
            src_ref=a, dst_ref=b, send_sem=send, recv_sem=recv, device_id=device, device_id_type=MESH
        )

    low, high = pl.ds(PAD, REACH), pl.ds(PAD + rows - REACH, REACH)
    halo_low, halo_high = pl.ds(PAD - REACH, REACH), pl.ds(PAD + rows, REACH)
    to_before, to_after, to_west, to_east, to_ocean = [], [], [], [], []
    for s in range(steps):
        to_before.append(
            remote(ext.at[s, :, low, :], ext.at[s, :, halo_high, :], lat_send.at[s, 0], lat_recv.at[s, 0], before)
        )
        to_after.append(
            remote(ext.at[s, :, high, :], ext.at[s, :, halo_low, :], lat_send.at[s, 1], lat_recv.at[s, 1], after)
        )
        to_west.append(remote(lon_out.at[s], lon_in.at[s, 0], lon_send.at[s, 0], lon_recv.at[s, 0], west))
        to_east.append(remote(lon_out.at[s], lon_in.at[s, 1], lon_send.at[s, 1], lon_recv.at[s, 1], east))
        to_ocean.append(remote(flux.at[s], src.at[s], flux_send.at[s], flux_recv.at[s], partner))

    barrier = pltpu.get_barrier_semaphore()
    for side in (west, east):
        pl.semaphore_signal(barrier, inc=1, device_id=side, device_id_type=MESH)
    for copy in load_state:
        copy.start()

    @pl.when(has_before)
    def _():
        pl.semaphore_signal(barrier, inc=1, device_id=before, device_id_type=MESH)

    @pl.when(has_after)
    def _():
        pl.semaphore_signal(barrier, inc=1, device_id=after, device_id_type=MESH)

    @pl.when(is_ocean)
    def _():
        pl.semaphore_signal(barrier, inc=1, device_id=partner, device_id_type=MESH)

    @pl.when(is_atmosphere)
    def _():
        for copy in sources:
            copy.start()

    for copy in load_regrid + load_rest:
        copy.start()

    lane = lax.broadcasted_iota(jnp.int32, (rows, cols), 1)

    def pack(packed, level, x):
        turned = pltpu.roll(x, (4 * level + REACH) % cols, 1)
        return jnp.where((lane >= 4 * level) & (lane < 4 * level + 4), turned, packed)

    for copy in load_state:
        copy.wait()
    packed = jnp.zeros((rows, cols), jnp.float32)
    for level in range(levels):
        packed = pack(packed, level, ext[0, level, own, :])
    lon_out[0] = packed
    nothing = jnp.zeros((steps, levels, REACH, cols), jnp.float32)

    @pl.when(jnp.logical_not(has_before))
    def _():
        ext[:, :, halo_low, :] = nothing

    @pl.when(jnp.logical_not(has_after))
    def _():
        ext[:, :, halo_high, :] = nothing

    edges = has_before.astype(jnp.int32) + has_after.astype(jnp.int32)
    pl.semaphore_wait(barrier, 2 + edges + is_atmosphere.astype(jnp.int32))

    def send_halo(s):
        to_west[s].start()
        to_east[s].start()

        @pl.when(has_before)
        def _():
            to_before[s].start()

        @pl.when(has_after)
        def _():
            to_after[s].start()

    send_halo(0)
    for copy in load_regrid:
        copy.wait()
    rate = cpl[...] * sea[...].astype(jnp.float32)

    @pl.when(is_atmosphere)
    def _():
        sources[0].wait()
        flux[0] = rate * (regrid(src.at[0], idx, wgt) - ext[0, 0, own, :])
        to_ocean[0].start()

    for copy in load_rest:
        copy.wait()
    east_speed, north_speed = vel[0] * (1.0 / 12.0), vel[1] * (1.0 / 12.0)
    centre = 1.0 - 4.0 * SMOOTHING
    lon_m2, lon_m1 = -east_speed, SMOOTHING + 8.0 * east_speed
    lon_p1, lon_p2 = SMOOTHING - 8.0 * east_speed, east_speed
    lat_m2, lat_m1 = -north_speed, SMOOTHING + 8.0 * north_speed
    lat_p1, lat_p2 = SMOOTHING - 8.0 * north_speed, north_speed
    own_m2, own_m1 = jnp.where(lane < 2, 0.0, lon_m2), jnp.where(lane < 1, 0.0, lon_m1)
    own_p1 = jnp.where(lane >= cols - 1, 0.0, lon_p1)
    own_p2 = jnp.where(lane >= cols - 2, 0.0, lon_p2)
    place = lax.bitwise_and(lane, 3)
    rim = lax.bitwise_and(place + (cols - REACH), cols - 1)
    spread = lambda c, keep: jnp.where(keep, lane_gather(c, rim), 0.0)
    rim_p2 = spread(lon_p2, place < 2)
    rim_p1 = spread(lon_p1, place == 1)
    rim_m2 = spread(lon_m2, place >= 2)
    rim_m1 = spread(lon_m1, place == 2)
    on_rim = (lane < REACH) | (lane >= cols - REACH)

    inverse, ratio = [None] * levels, [None] * levels
    for level in range(levels - 1, -1, -1):
        pivot = 1.0
        if level < levels - 1:
            pivot = pivot + mix[level] * (1.0 - ratio[level + 1])
        if level > 0:
            pivot = pivot + mix[level - 1]
        inverse[level] = 1.0 / pivot
        if level > 0:
            ratio[level] = mix[level - 1] * inverse[level]

    def own_part(s):
        for level in range(levels):
            x = ext[s, level, own, :]
            y[level] = (
                centre * x
                + own_m2 * pltpu.roll(x, 2, 1)
                + own_m1 * pltpu.roll(x, 1, 1)
                + own_p1 * pltpu.roll(x, cols - 1, 1)
                + own_p2 * pltpu.roll(x, cols - 2, 1)
            )

    for s in range(steps):
        own_part(s)
        if s + 1 < steps:

            @pl.when(is_atmosphere)
            def _():
                sources[s + 1].wait()
                part[s + 1] = regrid(src.at[s + 1], idx, wgt)

        @pl.when(is_ocean)
        def _():
            to_ocean[s].wait_recv()
            part[s] = rate * regrid(src.at[s], idx, wgt)

        @pl.when(has_after)
        def _():
            to_before[s].wait_recv()

        @pl.when(has_before)
        def _():
            to_after[s].wait_recv()

        to_west[s].wait_recv()
        to_east[s].wait_recv()
        from_east, from_west = lon_in[s, 0], lon_in[s, 1]
        rims = (
            rim_p2 * pltpu.roll(from_east, cols - 2, 1)
            + rim_p1 * pltpu.roll(from_east, cols - 1, 1)
            + rim_m2 * pltpu.roll(from_west, 2, 1)
            + rim_m1 * pltpu.roll(from_west, 1, 1)
        )
        values = [None] * levels
        for level in range(levels - 1, -1, -1):
            total = (
                y[level]
                + lat_m2 * ext[s, level, pl.ds(PAD - 2, rows), :]
                + lat_m1 * ext[s, level, pl.ds(PAD - 1, rows), :]
                + lat_p1 * ext[s, level, pl.ds(PAD + 1, rows), :]
                + lat_p2 * ext[s, level, pl.ds(PAD + 2, rows), :]
                + jnp.where(on_rim, pltpu.roll(rims, (cols - REACH - 4 * level) % cols, 1), 0.0)
            )
            if level < levels - 1:
                total = total + mix[level] * values[level + 1]
            if level > 0:
                values[level] = total * inverse[level]
            else:
                y[0] = total

        forcing = jnp.where(is_atmosphere, flux[s], part[s])
        x = (y[0] + forcing) * inverse[0]
        series[0, s] = jnp.where(is_atmosphere, forcing, x)
        last = s + 1 == steps
        if not last:

            @pl.when(is_atmosphere)
            def _():
                flux[s + 1] = rate * (part[s + 1] - x)
                to_ocean[s + 1].start()

        packed = jnp.zeros((rows, cols), jnp.float32)
        for level in range(levels):
            if level > 0:
                x = values[level] + ratio[level] * x
            if last:
                new_state[0, level] = x
            else:
                ext[s + 1, level, own, :] = x
                packed = pack(packed, level, x)
        if not last:
            lon_out[s + 1] = packed
            send_halo(s + 1)

    for s in range(steps):

        @pl.when(is_atmosphere)
        def _():
            to_ocean[s].wait_send()

        @pl.when(has_before)
        def _():
            to_before[s].wait_send()

        @pl.when(has_after)
        def _():
            to_after[s].wait_send()

        to_west[s].wait_send()
        to_east[s].wait_send()


def hand_over(state_in, series_in, state_out, series_out, sem):
    levels = state_in.shape[1]
    group = pl.cdiv(levels, GROUPS)
    copies = [pltpu.make_async_copy(series_in, series_out, sem.at[GROUPS])]
    for i, first in enumerate(range(0, levels, group)):
        some = pl.ds(first, min(group, levels - first))
        copies.append(pltpu.make_async_copy(state_in.at[0, some], state_out.at[0, some], sem.at[i]))
    for copy in copies:
        copy.start()
    for copy in copies:
        copy.wait()


def per_device(n_lat, n_lon, state, prev, mixing, velocity, coupling, sea_mask, index, weight):
    levels, rows, cols = state.shape[1:]
    steps, points = prev.shape[0], index.shape[1]
    tile = (rows, cols)
    floats = lambda *lead: pltpu.VMEM(lead + tile, jnp.float32)
    dma = pltpu.SemaphoreType.DMA
    shapes = (
        jax.ShapeDtypeStruct(state.shape, jnp.float32),
        jax.ShapeDtypeStruct((1, steps) + tile, jnp.float32),
    )
    outs = pl.pallas_call(
        functools.partial(kernel, (n_lat, n_lon, steps, levels, rows, cols)),
        out_shape=tuple(pltpu.VMEM(s.shape, s.dtype) for s in shapes),
        in_specs=[pl.BlockSpec(memory_space=pltpu.HBM)] * 8,
        out_specs=[pl.BlockSpec(memory_space=pltpu.VMEM)] * 2,
        scratch_shapes=[
            pltpu.VMEM((steps, levels, rows + 2 * PAD, cols), jnp.float32),
            floats(steps),
            floats(levels - 1),
            floats(2),
            floats(),
            pltpu.VMEM(tile, jnp.int32),
            pltpu.VMEM((points,) + tile, jnp.int32),
            floats(points),
            floats(steps),
            floats(steps),
            floats(levels),
            floats(steps),
            floats(steps, 2),
            dma((3 * GROUPS + 1,)),
            dma((steps,)),
            dma((steps, 2)),
            dma((steps, 2)),
            dma((steps, 2)),
            dma((steps, 2)),
            dma((steps,)),
            dma((steps,)),
        ],
        compiler_params=pltpu.CompilerParams(collective_id=0, has_side_effects=True, vmem_limit_bytes=VMEM_BYTES),
        name="coupled_window",
    )(*(pltpu.with_memory_space_constraint(a, pltpu.HBM) for a in (state, prev, mixing, velocity, coupling, sea_mask, index, weight)))
    return pl.pallas_call(
        hand_over,
        out_shape=shapes,
        in_specs=[pl.BlockSpec(memory_space=pltpu.VMEM)] * 2,
        out_specs=[pl.BlockSpec(memory_space=pl.ANY)] * 2,
        scratch_shapes=[dma((GROUPS + 1,))],
        compiler_params=pltpu.CompilerParams(vmem_limit_bytes=VMEM_BYTES),
        name="hand_over",
    )(*outs)


def solution(mesh):
    in_specs = (
        P("comp", None, "lat", "lon"),
        P(None, "lat", "lon"),
        P("comp", None, "lat", "lon"),
        P("comp", None, "lat", "lon"),
        P("comp", "lat", "lon"),
        P("comp", "lat", "lon"),
        P("comp", None, "lat", "lon"),
        P("comp", None, "lat", "lon"),
    )
    out_specs = (P("comp", None, "lat", "lon"), P("comp", None, "lat", "lon"))
    return jax.shard_map(
        functools.partial(per_device, mesh.shape["lat"], mesh.shape["lon"]),
        mesh=mesh,
        in_specs=in_specs,
        out_specs=out_specs,
        check_vma=False,
    )
```

```python
import functools

import jax
import jax.numpy as jnp
from jax import lax
from jax.experimental import pallas as pl
from jax.experimental.pallas import tpu as pltpu
from jax.sharding import PartitionSpec as P

SMOOTHING = 0.15
MESH = pl.DeviceIdType.MESH
PAD = 8
REACH = 2
VMEM_BYTES = 8 * 2**20
GROUPS = 4
SUB = 8


def lane_gather(values, lanes):
    return jnp.take_along_axis(values, lanes, axis=1, mode="promise_in_bounds")


def regrid(source, index, weight):
    points, rows, cols = index.shape
    shift = cols.bit_length() - 1
    parts = []
    for top in range(0, rows, SUB):
        total = jnp.zeros((SUB, cols), jnp.float32)
        for j in range(points):
            where = index[j, top : top + SUB, :]
            lanes, owner = lax.bitwise_and(where, cols - 1), lax.shift_right_logical(where, shift)
            picked = jnp.zeros((SUB, cols), jnp.float32)
            for row in range(rows):
                line = jnp.broadcast_to(source[row : row + 1, :], (SUB, cols))
                picked = jnp.where(owner == row, lane_gather(line, lanes), picked)
            total = total + weight[j, top : top + SUB, :] * picked
        parts.append(total)
    return jnp.concatenate(parts, axis=0)


def kernel(
    sizes,
    state,
    prev,
    mixing,
    velocity,
    coupling,
    sea_mask,
    interp_index,
    interp_weight,
    new_state,
    series,
    ext,
    src,
    mix,
    vel,
    cpl,
    sea,
    idx,
    wgt,
    part,
    flux,
    y,
    lat_out,
    lat_in,
    lon_out,
    lon_in,
    in_sem,
    src_sem,
    lat_send,
    lat_recv,
    lon_send,
    lon_recv,
    flux_send,
    flux_recv,
):
    n_lat, n_lon, steps, levels, rows, cols = sizes
    comp, lat, lon = (lax.axis_index(a) for a in ("comp", "lat", "lon"))
    is_atmosphere = comp == 0
    is_ocean = comp != 0
    has_before = lat > 0
    has_after = lat < n_lat - 1
    before, after = {"lat": lat - 1}, {"lat": lat + 1}
    west, east = {"lon": lax.rem(lon + n_lon - 1, n_lon)}, {"lon": lax.rem(lon + 1, n_lon)}
    partner = {"comp": 1 - comp}
    own = pl.ds(PAD, rows)

    def chunks(count):
        size = pl.cdiv(count, GROUPS)
        return [pl.ds(first, min(size, count - first)) for first in range(0, count, size)]

    count = iter(range(3 * GROUPS + 1))
    load = lambda a, b: pltpu.make_async_copy(a, b, in_sem.at[next(count)])
    load_state = [load(state.at[0, c], ext.at[0, c, own, :]) for c in chunks(levels)]
    load_regrid = [
        load(a.at[0], b) for a, b in ((interp_index, idx), (interp_weight, wgt), (coupling, cpl), (sea_mask, sea))
    ]
    load_rest = [load(velocity.at[0], vel)]
    load_rest += [load(mixing.at[0, c], mix.at[c]) for c in chunks(levels - 1)]
    sources = [pltpu.make_async_copy(prev.at[s], src.at[s], src_sem.at[s]) for s in range(steps)]

    def remote(a, b, send, recv, device):
        return pltpu.make_async_remote_copy(
            src_ref=a, dst_ref=b, send_sem=send, recv_sem=recv, device_id=device, device_id_type=MESH
        )

    halo_low, halo_high = pl.ds(PAD - REACH, REACH), pl.ds(PAD + rows, REACH)
    to_before, to_after, to_west, to_east, to_ocean = [], [], [], [], []
    for s in range(steps):
        to_before.append(remote(lat_out.at[s, 0], lat_in.at[s, 0], lat_send.at[s, 0], lat_recv.at[s, 0], before))
        to_after.append(remote(lat_out.at[s, 1], lat_in.at[s, 1], lat_send.at[s, 1], lat_recv.at[s, 1], after))
        to_west.append(remote(lon_out.at[s], lon_in.at[s, 0], lon_send.at[s, 0], lon_recv.at[s, 0], west))
        to_east.append(remote(lon_out.at[s], lon_in.at[s, 1], lon_send.at[s, 1], lon_recv.at[s, 1], east))
        to_ocean.append(remote(flux.at[s], src.at[s], flux_send.at[s], flux_recv.at[s], partner))

    barrier = pltpu.get_barrier_semaphore()
    for side in (west, east):
        pl.semaphore_signal(barrier, inc=1, device_id=side, device_id_type=MESH)
    for copy in load_state:
        copy.start()

    @pl.when(has_before)
    def _():
        pl.semaphore_signal(barrier, inc=1, device_id=before, device_id_type=MESH)

    @pl.when(has_after)
    def _():
        pl.semaphore_signal(barrier, inc=1, device_id=after, device_id_type=MESH)

    @pl.when(is_ocean)
    def _():
        pl.semaphore_signal(barrier, inc=1, device_id=partner, device_id_type=MESH)

    @pl.when(is_atmosphere)
    def _():
        for copy in sources:
            copy.start()

    for copy in load_regrid + load_rest:
        copy.start()

    lane = lax.broadcasted_iota(jnp.int32, (rows, cols), 1)

    def pack(packed, level, x):
        turned = pltpu.roll(x, (4 * level + REACH) % cols, 1)
        return jnp.where((lane >= 4 * level) & (lane < 4 * level + 4), turned, packed)

    def pack_lat(s, level, x):
        lat_out[s, 0, pl.ds(REACH * level, REACH), :] = x[:REACH]
        lat_out[s, 1, pl.ds(REACH * level, REACH), :] = x[rows - REACH :]

    for copy in load_state:
        copy.wait()
    packed = jnp.zeros((rows, cols), jnp.float32)
    for level in range(levels):
        x = ext[0, level, own, :]
        packed = pack(packed, level, x)
        pack_lat(0, level, x)
    lon_out[0] = packed
    nothing = jnp.zeros((steps, levels, REACH, cols), jnp.float32)

    @pl.when(jnp.logical_not(has_before))
    def _():
        ext[:, :, halo_low, :] = nothing

    @pl.when(jnp.logical_not(has_after))
    def _():
        ext[:, :, halo_high, :] = nothing

    edges = has_before.astype(jnp.int32) + has_after.astype(jnp.int32)
    pl.semaphore_wait(barrier, 2 + edges + is_atmosphere.astype(jnp.int32))

    def send_halo(s):
        @pl.when(has_before)
        def _():
            to_before[s].start()

        @pl.when(has_after)
        def _():
            to_after[s].start()

        to_west[s].start()
        to_east[s].start()

    send_halo(0)
    for copy in load_regrid:
        copy.wait()
    rate = cpl[...] * sea[...].astype(jnp.float32)

    @pl.when(is_atmosphere)
    def _():
        sources[0].wait()
        flux[0] = rate * (regrid(src.at[0], idx, wgt) - ext[0, 0, own, :])
        to_ocean[0].start()

    for copy in load_rest:
        copy.wait()
    east_speed, north_speed = vel[0] * (1.0 / 12.0), vel[1] * (1.0 / 12.0)
    centre = 1.0 - 4.0 * SMOOTHING
    lon_m2, lon_m1 = -east_speed, SMOOTHING + 8.0 * east_speed
    lon_p1, lon_p2 = SMOOTHING - 8.0 * east_speed, east_speed
    lat_m2, lat_m1 = -north_speed, SMOOTHING + 8.0 * north_speed
    lat_p1, lat_p2 = SMOOTHING - 8.0 * north_speed, north_speed
    own_m2, own_m1 = jnp.where(lane < 2, 0.0, lon_m2), jnp.where(lane < 1, 0.0, lon_m1)
    own_p1 = jnp.where(lane >= cols - 1, 0.0, lon_p1)
    own_p2 = jnp.where(lane >= cols - 2, 0.0, lon_p2)
    place = lax.bitwise_and(lane, 3)
    rim = lax.bitwise_and(place + (cols - REACH), cols - 1)
    spread = lambda c, keep: jnp.where(keep, lane_gather(c, rim), 0.0)
    rim_p2 = spread(lon_p2, place < 2)
    rim_p1 = spread(lon_p1, place == 1)
    rim_m2 = spread(lon_m2, place >= 2)
    rim_m1 = spread(lon_m1, place == 2)
    on_rim = (lane < REACH) | (lane >= cols - REACH)

    inverse, ratio = [None] * levels, [None] * levels
    for level in range(levels - 1, -1, -1):
        pivot = 1.0
        if level < levels - 1:
            pivot = pivot + mix[level] * (1.0 - ratio[level + 1])
        if level > 0:
            pivot = pivot + mix[level - 1]
        inverse[level] = 1.0 / pivot
        if level > 0:
            ratio[level] = mix[level - 1] * inverse[level]

    def own_part(s):
        for level in range(levels):
            x = ext[s, level, own, :]
            y[level] = (
                centre * x
                + own_m2 * pltpu.roll(x, 2, 1)
                + own_m1 * pltpu.roll(x, 1, 1)
                + own_p1 * pltpu.roll(x, cols - 1, 1)
                + own_p2 * pltpu.roll(x, cols - 2, 1)
            )

    for s in range(steps):
        own_part(s)
        if s + 1 < steps:

            @pl.when(is_atmosphere)
            def _():
                sources[s + 1].wait()
                part[s + 1] = regrid(src.at[s + 1], idx, wgt)

        @pl.when(is_ocean)
        def _():
            to_ocean[s].wait_recv()
            part[s] = rate * regrid(src.at[s], idx, wgt)

        @pl.when(has_after)
        def _():
            to_before[s].wait_recv()
            for level in range(levels):
                ext[s, level, halo_high, :] = lat_in[s, 0, pl.ds(REACH * level, REACH), :]

        @pl.when(has_before)
        def _():
            to_after[s].wait_recv()
            for level in range(levels):
                ext[s, level, halo_low, :] = lat_in[s, 1, pl.ds(REACH * level, REACH), :]

        to_west[s].wait_recv()
        to_east[s].wait_recv()
        from_east, from_west = lon_in[s, 0], lon_in[s, 1]
        rims = (
            rim_p2 * pltpu.roll(from_east, cols - 2, 1)
            + rim_p1 * pltpu.roll(from_east, cols - 1, 1)
            + rim_m2 * pltpu.roll(from_west, 2, 1)
            + rim_m1 * pltpu.roll(from_west, 1, 1)
        )
        values = [None] * levels
        for level in range(levels - 1, -1, -1):
            total = (
                y[level]
                + lat_m2 * ext[s, level, pl.ds(PAD - 2, rows), :]
                + lat_m1 * ext[s, level, pl.ds(PAD - 1, rows), :]
                + lat_p1 * ext[s, level, pl.ds(PAD + 1, rows), :]
                + lat_p2 * ext[s, level, pl.ds(PAD + 2, rows), :]
                + jnp.where(on_rim, pltpu.roll(rims, (cols - REACH - 4 * level) % cols, 1), 0.0)
            )
            if level < levels - 1:
                total = total + mix[level] * values[level + 1]
            if level > 0:
                values[level] = total * inverse[level]
            else:
                y[0] = total

        forcing = jnp.where(is_atmosphere, flux[s], part[s])
        x = (y[0] + forcing) * inverse[0]
        series[0, s] = jnp.where(is_atmosphere, forcing, x)
        last = s + 1 == steps
        if not last:

            @pl.when(is_atmosphere)
            def _():
                flux[s + 1] = rate * (part[s + 1] - x)
                to_ocean[s + 1].start()

        packed = jnp.zeros((rows, cols), jnp.float32)
        for level in range(levels):
            if level > 0:
                x = values[level] + ratio[level] * x
            if last:
                new_state[0, level] = x
            else:
                ext[s + 1, level, own, :] = x
                packed = pack(packed, level, x)
                pack_lat(s + 1, level, x)
        if not last:
            lon_out[s + 1] = packed
            send_halo(s + 1)

    for s in range(steps):

        @pl.when(is_atmosphere)
        def _():
            to_ocean[s].wait_send()

        @pl.when(has_before)
        def _():
            to_before[s].wait_send()

        @pl.when(has_after)
        def _():
            to_after[s].wait_send()

        to_west[s].wait_send()
        to_east[s].wait_send()


def hand_over(state_in, series_in, state_out, series_out, sem):
    levels = state_in.shape[1]
    group = pl.cdiv(levels, GROUPS)
    copies = [pltpu.make_async_copy(series_in, series_out, sem.at[GROUPS])]
    for i, first in enumerate(range(0, levels, group)):
        some = pl.ds(first, min(group, levels - first))
        copies.append(pltpu.make_async_copy(state_in.at[0, some], state_out.at[0, some], sem.at[i]))
    for copy in copies:
        copy.start()
    for copy in copies:
        copy.wait()


def per_device(n_lat, n_lon, state, prev, mixing, velocity, coupling, sea_mask, index, weight):
    levels, rows, cols = state.shape[1:]
    steps, points = prev.shape[0], index.shape[1]
    tile = (rows, cols)
    floats = lambda *lead: pltpu.VMEM(lead + tile, jnp.float32)
    dma = pltpu.SemaphoreType.DMA
    shapes = (
        jax.ShapeDtypeStruct(state.shape, jnp.float32),
        jax.ShapeDtypeStruct((1, steps) + tile, jnp.float32),
    )
    outs = pl.pallas_call(
        functools.partial(kernel, (n_lat, n_lon, steps, levels, rows, cols)),
        out_shape=tuple(pltpu.VMEM(s.shape, s.dtype) for s in shapes),
        in_specs=[pl.BlockSpec(memory_space=pltpu.HBM)] * 8,
        out_specs=[pl.BlockSpec(memory_space=pltpu.VMEM)] * 2,
        scratch_shapes=[
            pltpu.VMEM((steps, levels, rows + 2 * PAD, cols), jnp.float32),
            floats(steps),
            floats(levels - 1),
            floats(2),
            floats(),
            pltpu.VMEM(tile, jnp.int32),
            pltpu.VMEM((points,) + tile, jnp.int32),
            floats(points),
            floats(steps),
            floats(steps),
            floats(levels),
            pltpu.VMEM((steps, 2, levels * REACH, cols), jnp.float32),
            pltpu.VMEM((steps, 2, levels * REACH, cols), jnp.float32),
            floats(steps),
            floats(steps, 2),
            dma((3 * GROUPS + 1,)),
            dma((steps,)),
            dma((steps, 2)),
            dma((steps, 2)),
            dma((steps, 2)),
            dma((steps, 2)),
            dma((steps,)),
            dma((steps,)),
        ],
        compiler_params=pltpu.CompilerParams(collective_id=0, has_side_effects=True, vmem_limit_bytes=VMEM_BYTES),
        name="coupled_window",
    )(*(pltpu.with_memory_space_constraint(a, pltpu.HBM) for a in (state, prev, mixing, velocity, coupling, sea_mask, index, weight)))
    return pl.pallas_call(
        hand_over,
        out_shape=shapes,
        in_specs=[pl.BlockSpec(memory_space=pltpu.VMEM)] * 2,
        out_specs=[pl.BlockSpec(memory_space=pl.ANY)] * 2,
        scratch_shapes=[dma((GROUPS + 1,))],
        compiler_params=pltpu.CompilerParams(vmem_limit_bytes=VMEM_BYTES),
        name="hand_over",
    )(*outs)


def solution(mesh):
    in_specs = (
        P("comp", None, "lat", "lon"),
        P(None, "lat", "lon"),
        P("comp", None, "lat", "lon"),
        P("comp", None, "lat", "lon"),
        P("comp", "lat", "lon"),
        P("comp", "lat", "lon"),
        P("comp", None, "lat", "lon"),
        P("comp", None, "lat", "lon"),
    )
    out_specs = (P("comp", None, "lat", "lon"), P("comp", None, "lat", "lon"))
    return jax.shard_map(
        functools.partial(per_device, mesh.shape["lat"], mesh.shape["lon"]),
        mesh=mesh,
        in_specs=in_specs,
        out_specs=out_specs,
        check_vma=False,
    )
```

```python
import functools

import jax
import jax.numpy as jnp
from jax import lax
from jax.experimental import pallas as pl
from jax.experimental.pallas import tpu as pltpu
from jax.sharding import PartitionSpec as P

SMOOTHING = 0.15
MESH = pl.DeviceIdType.MESH
PAD = 8
REACH = 2
VMEM_BYTES = 8 * 2**20
GROUPS = 4
SUB = 8


def lane_gather(values, lanes):
    return jnp.take_along_axis(values, lanes, axis=1, mode="promise_in_bounds")


def regrid(source, index, weight):
    points, rows, cols = index.shape
    shift = cols.bit_length() - 1
    parts = []
    for top in range(0, rows, SUB):
        total = jnp.zeros((SUB, cols), jnp.float32)
        for j in range(points):
            where = index[j, top : top + SUB, :]
            lanes, owner = lax.bitwise_and(where, cols - 1), lax.shift_right_logical(where, shift)
            picked = jnp.zeros((SUB, cols), jnp.float32)
            for row in range(rows):
                line = jnp.broadcast_to(source[row : row + 1, :], (SUB, cols))
                picked = jnp.where(owner == row, lane_gather(line, lanes), picked)
            total = total + weight[j, top : top + SUB, :] * picked
        parts.append(total)
    return jnp.concatenate(parts, axis=0)


def kernel(
    sizes,
    state,
    prev,
    mixing,
    velocity,
    coupling,
    sea_mask,
    interp_index,
    interp_weight,
    new_state,
    series,
    ext,
    src,
    mix,
    vel,
    cpl,
    sea,
    idx,
    wgt,
    part,
    flux,
    y,
    lat_out,
    lat_in,
    lon_out,
    lon_in,
    in_sem,
    src_sem,
    lat_send,
    lat_recv,
    lon_send,
    lon_recv,
    flux_send,
    flux_recv,
):
    n_lat, n_lon, steps, levels, rows, cols = sizes
    comp, lat, lon = (lax.axis_index(a) for a in ("comp", "lat", "lon"))
    is_atmosphere = comp == 0
    is_ocean = comp != 0
    has_before = lat > 0
    has_after = lat < n_lat - 1
    before, after = {"lat": lat - 1}, {"lat": lat + 1}
    west, east = {"lon": lax.rem(lon + n_lon - 1, n_lon)}, {"lon": lax.rem(lon + 1, n_lon)}
    partner = {"comp": 1 - comp}
    own = pl.ds(PAD, rows)

    def chunks(count):
        size = pl.cdiv(count, GROUPS)
        return [pl.ds(first, min(size, count - first)) for first in range(0, count, size)]

    count = iter(range(3 * GROUPS + 1))
    load = lambda a, b: pltpu.make_async_copy(a, b, in_sem.at[next(count)])
    load_state = [load(state.at[0, c], ext.at[0, c, own, :]) for c in chunks(levels)]
    load_regrid = [
        load(a.at[0], b) for a, b in ((interp_index, idx), (interp_weight, wgt), (coupling, cpl), (sea_mask, sea))
    ]
    load_rest = [load(velocity.at[0], vel)]
    load_rest += [load(mixing.at[0, c], mix.at[c]) for c in chunks(levels - 1)]
    sources = [pltpu.make_async_copy(prev.at[s], src.at[s], src_sem.at[s]) for s in range(steps)]

    def remote(a, b, send, recv, device):
        return pltpu.make_async_remote_copy(
            src_ref=a, dst_ref=b, send_sem=send, recv_sem=recv, device_id=device, device_id_type=MESH
        )

    halo_low, halo_high = pl.ds(PAD - REACH, REACH), pl.ds(PAD + rows, REACH)
    to_before, to_after, to_west, to_east, to_ocean = [], [], [], [], []
    for s in range(steps):
        to_before.append(remote(lat_out.at[s, 0], lat_in.at[s, 0], lat_send.at[s, 0], lat_recv.at[s, 0], before))
        to_after.append(remote(lat_out.at[s, 1], lat_in.at[s, 1], lat_send.at[s, 1], lat_recv.at[s, 1], after))
        to_west.append(remote(lon_out.at[s], lon_in.at[s, 0], lon_send.at[s, 0], lon_recv.at[s, 0], west))
        to_east.append(remote(lon_out.at[s], lon_in.at[s, 1], lon_send.at[s, 1], lon_recv.at[s, 1], east))
        to_ocean.append(remote(flux.at[s], src.at[s], flux_send.at[s], flux_recv.at[s], partner))

    barrier = pltpu.get_barrier_semaphore()
    for side in (west, east):
        pl.semaphore_signal(barrier, inc=1, device_id=side, device_id_type=MESH)
    for copy in load_state:
        copy.start()

    @pl.when(has_before)
    def _():
        pl.semaphore_signal(barrier, inc=1, device_id=before, device_id_type=MESH)

    @pl.when(has_after)
    def _():
        pl.semaphore_signal(barrier, inc=1, device_id=after, device_id_type=MESH)

    @pl.when(is_ocean)
    def _():
        pl.semaphore_signal(barrier, inc=1, device_id=partner, device_id_type=MESH)

    @pl.when(is_atmosphere)
    def _():
        for copy in sources:
            copy.start()

    for copy in load_regrid + load_rest:
        copy.start()

    lane = lax.broadcasted_iota(jnp.int32, (rows, cols), 1)

    def pack(packed, level, x):
        turned = pltpu.roll(x, (4 * level + REACH) % cols, 1)
        return jnp.where((lane >= 4 * level) & (lane < 4 * level + 4), turned, packed)

    def pack_lat(s, level, x):
        lat_out[s, 0, pl.ds(REACH * level, REACH), :] = x[:REACH]
        lat_out[s, 1, pl.ds(REACH * level, REACH), :] = x[rows - REACH :]

    for copy in load_state:
        copy.wait()
    packed = jnp.zeros((rows, cols), jnp.float32)
    for level in range(levels):
        x = ext[0, level, own, :]
        packed = pack(packed, level, x)
        pack_lat(0, level, x)
    lon_out[0] = packed
    nothing = jnp.zeros((steps, levels, REACH, cols), jnp.float32)

    @pl.when(jnp.logical_not(has_before))
    def _():
        ext[:, :, halo_low, :] = nothing

    @pl.when(jnp.logical_not(has_after))
    def _():
        ext[:, :, halo_high, :] = nothing

    edges = has_before.astype(jnp.int32) + has_after.astype(jnp.int32)
    pl.semaphore_wait(barrier, 2 + edges + is_atmosphere.astype(jnp.int32))

    def send_halo(s):
        @pl.when(has_before)
        def _():
            to_before[s].start()

        @pl.when(has_after)
        def _():
            to_after[s].start()

        to_west[s].start()
        to_east[s].start()

    send_halo(0)
    for copy in load_regrid:
        copy.wait()
    rate = cpl[...] * sea[...].astype(jnp.float32)

    @pl.when(is_atmosphere)
    def _():
        sources[0].wait()
        flux[0] = rate * (regrid(src.at[0], idx, wgt) - ext[0, 0, own, :])
        to_ocean[0].start()

    for copy in load_rest:
        copy.wait()
    east_speed, north_speed = vel[0] * (1.0 / 12.0), vel[1] * (1.0 / 12.0)
    centre = 1.0 - 4.0 * SMOOTHING
    lon_m2, lon_m1 = -east_speed, SMOOTHING + 8.0 * east_speed
    lon_p1, lon_p2 = SMOOTHING - 8.0 * east_speed, east_speed
    lat_m2, lat_m1 = -north_speed, SMOOTHING + 8.0 * north_speed
    lat_p1, lat_p2 = SMOOTHING - 8.0 * north_speed, north_speed
    own_m2, own_m1 = jnp.where(lane < 2, 0.0, lon_m2), jnp.where(lane < 1, 0.0, lon_m1)
    own_p1 = jnp.where(lane >= cols - 1, 0.0, lon_p1)
    own_p2 = jnp.where(lane >= cols - 2, 0.0, lon_p2)
    place = lax.bitwise_and(lane, 3)
    rim = lax.bitwise_and(place + (cols - REACH), cols - 1)
    spread = lambda c, keep: jnp.where(keep, lane_gather(c, rim), 0.0)
    rim_p2 = spread(lon_p2, place < 2)
    rim_p1 = spread(lon_p1, place == 1)
    rim_m2 = spread(lon_m2, place >= 2)
    rim_m1 = spread(lon_m1, place == 2)
    on_rim = (lane < REACH) | (lane >= cols - REACH)

    inverse, ratio = [None] * levels, [None] * levels
    for level in range(levels - 1, -1, -1):
        pivot = 1.0
        if level < levels - 1:
            pivot = pivot + mix[level] * (1.0 - ratio[level + 1])
        if level > 0:
            pivot = pivot + mix[level - 1]
        inverse[level] = 1.0 / pivot
        if level > 0:
            ratio[level] = mix[level - 1] * inverse[level]

    def own_part(s):
        for level in range(levels):
            x = ext[s, level, own, :]
            y[level] = (
                centre * x
                + own_m2 * pltpu.roll(x, 2, 1)
                + own_m1 * pltpu.roll(x, 1, 1)
                + own_p1 * pltpu.roll(x, cols - 1, 1)
                + own_p2 * pltpu.roll(x, cols - 2, 1)
            )

    for s in range(steps):
        own_part(s)
        @pl.when(is_ocean)
        def _():
            to_ocean[s].wait_recv()
            part[s] = rate * regrid(src.at[s], idx, wgt)

        @pl.when(has_after)
        def _():
            to_before[s].wait_recv()
            for level in range(levels):
                ext[s, level, halo_high, :] = lat_in[s, 0, pl.ds(REACH * level, REACH), :]

        @pl.when(has_before)
        def _():
            to_after[s].wait_recv()
            for level in range(levels):
                ext[s, level, halo_low, :] = lat_in[s, 1, pl.ds(REACH * level, REACH), :]

        to_west[s].wait_recv()
        to_east[s].wait_recv()
        from_east, from_west = lon_in[s, 0], lon_in[s, 1]
        rims = (
            rim_p2 * pltpu.roll(from_east, cols - 2, 1)
            + rim_p1 * pltpu.roll(from_east, cols - 1, 1)
            + rim_m2 * pltpu.roll(from_west, 2, 1)
            + rim_m1 * pltpu.roll(from_west, 1, 1)
        )
        values = [None] * levels
        for level in range(levels - 1, -1, -1):
            total = (
                y[level]
                + lat_m2 * ext[s, level, pl.ds(PAD - 2, rows), :]
                + lat_m1 * ext[s, level, pl.ds(PAD - 1, rows), :]
                + lat_p1 * ext[s, level, pl.ds(PAD + 1, rows), :]
                + lat_p2 * ext[s, level, pl.ds(PAD + 2, rows), :]
                + jnp.where(on_rim, pltpu.roll(rims, (cols - REACH - 4 * level) % cols, 1), 0.0)
            )
            if level < levels - 1:
                total = total + mix[level] * values[level + 1]
            if level > 0:
                values[level] = total * inverse[level]
            else:
                y[0] = total

        forcing = jnp.where(is_atmosphere, flux[s], part[s])
        x = (y[0] + forcing) * inverse[0]
        series[0, s] = jnp.where(is_atmosphere, forcing, x)
        last = s + 1 == steps
        packed = jnp.zeros((rows, cols), jnp.float32)
        for level in range(levels):
            if level > 0:
                x = values[level] + ratio[level] * x
            if last:
                new_state[0, level] = x
            else:
                ext[s + 1, level, own, :] = x
                packed = pack(packed, level, x)
                pack_lat(s + 1, level, x)
        if not last:
            lon_out[s + 1] = packed
            send_halo(s + 1)

            @pl.when(is_atmosphere)
            def _():
                sources[s + 1].wait()
                flux[s + 1] = rate * (regrid(src.at[s + 1], idx, wgt) - ext[s + 1, 0, own, :])
                to_ocean[s + 1].start()

    for s in range(steps):

        @pl.when(is_atmosphere)
        def _():
            to_ocean[s].wait_send()

        @pl.when(has_before)
        def _():
            to_before[s].wait_send()

        @pl.when(has_after)
        def _():
            to_after[s].wait_send()

        to_west[s].wait_send()
        to_east[s].wait_send()


def hand_over(state_in, series_in, state_out, series_out, sem):
    levels = state_in.shape[1]
    group = pl.cdiv(levels, GROUPS)
    copies = [pltpu.make_async_copy(series_in, series_out, sem.at[GROUPS])]
    for i, first in enumerate(range(0, levels, group)):
        some = pl.ds(first, min(group, levels - first))
        copies.append(pltpu.make_async_copy(state_in.at[0, some], state_out.at[0, some], sem.at[i]))
    for copy in copies:
        copy.start()
    for copy in copies:
        copy.wait()


def per_device(n_lat, n_lon, state, prev, mixing, velocity, coupling, sea_mask, index, weight):
    levels, rows, cols = state.shape[1:]
    steps, points = prev.shape[0], index.shape[1]
    tile = (rows, cols)
    floats = lambda *lead: pltpu.VMEM(lead + tile, jnp.float32)
    dma = pltpu.SemaphoreType.DMA
    shapes = (
        jax.ShapeDtypeStruct(state.shape, jnp.float32),
        jax.ShapeDtypeStruct((1, steps) + tile, jnp.float32),
    )
    outs = pl.pallas_call(
        functools.partial(kernel, (n_lat, n_lon, steps, levels, rows, cols)),
        out_shape=tuple(pltpu.VMEM(s.shape, s.dtype) for s in shapes),
        in_specs=[pl.BlockSpec(memory_space=pltpu.HBM)] * 8,
        out_specs=[pl.BlockSpec(memory_space=pltpu.VMEM)] * 2,
        scratch_shapes=[
            pltpu.VMEM((steps, levels, rows + 2 * PAD, cols), jnp.float32),
            floats(steps),
            floats(levels - 1),
            floats(2),
            floats(),
            pltpu.VMEM(tile, jnp.int32),
            pltpu.VMEM((points,) + tile, jnp.int32),
            floats(points),
            floats(steps),
            floats(steps),
            floats(levels),
            pltpu.VMEM((steps, 2, levels * REACH, cols), jnp.float32),
            pltpu.VMEM((steps, 2, levels * REACH, cols), jnp.float32),
            floats(steps),
            floats(steps, 2),
            dma((3 * GROUPS + 1,)),
            dma((steps,)),
            dma((steps, 2)),
            dma((steps, 2)),
            dma((steps, 2)),
            dma((steps, 2)),
            dma((steps,)),
            dma((steps,)),
        ],
        compiler_params=pltpu.CompilerParams(collective_id=0, has_side_effects=True, vmem_limit_bytes=VMEM_BYTES),
        name="coupled_window",
    )(*(pltpu.with_memory_space_constraint(a, pltpu.HBM) for a in (state, prev, mixing, velocity, coupling, sea_mask, index, weight)))
    return pl.pallas_call(
        hand_over,
        out_shape=shapes,
        in_specs=[pl.BlockSpec(memory_space=pltpu.VMEM)] * 2,
        out_specs=[pl.BlockSpec(memory_space=pl.ANY)] * 2,
        scratch_shapes=[dma((GROUPS + 1,))],
        compiler_params=pltpu.CompilerParams(vmem_limit_bytes=VMEM_BYTES),
        name="hand_over",
    )(*outs)


def solution(mesh):
    in_specs = (
        P("comp", None, "lat", "lon"),
        P(None, "lat", "lon"),
        P("comp", None, "lat", "lon"),
        P("comp", None, "lat", "lon"),
        P("comp", "lat", "lon"),
        P("comp", "lat", "lon"),
        P("comp", None, "lat", "lon"),
        P("comp", None, "lat", "lon"),
    )
    out_specs = (P("comp", None, "lat", "lon"), P("comp", None, "lat", "lon"))
    return jax.shard_map(
        functools.partial(per_device, mesh.shape["lat"], mesh.shape["lon"]),
        mesh=mesh,
        in_specs=in_specs,
        out_specs=out_specs,
        check_vma=False,
    )
```

```python
import functools

import jax
import jax.numpy as jnp
from jax import lax
from jax.experimental import pallas as pl
from jax.experimental.pallas import tpu as pltpu
from jax.sharding import PartitionSpec as P

SMOOTHING = 0.15
MESH = pl.DeviceIdType.MESH
PAD = 8
REACH = 2
VMEM_BYTES = 8 * 2**20
GROUPS = 4
SUB = 8


def lane_gather(values, lanes):
    return jnp.take_along_axis(values, lanes, axis=1, mode="promise_in_bounds")


def regrid(source, index, weight):
    points, rows, cols = index.shape
    shift = cols.bit_length() - 1
    parts = []
    for top in range(0, rows, SUB):
        total = jnp.zeros((SUB, cols), jnp.float32)
        for j in range(points):
            where = index[j, top : top + SUB, :]
            lanes, owner = lax.bitwise_and(where, cols - 1), lax.shift_right_logical(where, shift)
            picked = jnp.zeros((SUB, cols), jnp.float32)
            for row in range(rows):
                line = jnp.broadcast_to(source[row : row + 1, :], (SUB, cols))
                picked = jnp.where(owner == row, lane_gather(line, lanes), picked)
            total = total + weight[j, top : top + SUB, :] * picked
        parts.append(total)
    return jnp.concatenate(parts, axis=0)


def kernel(
    sizes,
    state,
    prev,
    mixing,
    velocity,
    coupling,
    sea_mask,
    interp_index,
    interp_weight,
    new_state,
    series,
    ext,
    src,
    mix,
    vel,
    cpl,
    sea,
    idx,
    wgt,
    part,
    flux,
    y,
    lat_out,
    lat_in,
    lon_out,
    lon_in,
    in_sem,
    src_sem,
    lat_send,
    lat_recv,
    lon_send,
    lon_recv,
    flux_send,
    flux_recv,
):
    n_lat, n_lon, steps, levels, rows, cols = sizes
    comp, lat, lon = (lax.axis_index(a) for a in ("comp", "lat", "lon"))
    is_atmosphere = comp == 0
    is_ocean = comp != 0
    has_before = lat > 0
    has_after = lat < n_lat - 1
    before, after = {"lat": lat - 1}, {"lat": lat + 1}
    west, east = {"lon": lax.rem(lon + n_lon - 1, n_lon)}, {"lon": lax.rem(lon + 1, n_lon)}
    partner = {"comp": 1 - comp}
    own = pl.ds(PAD, rows)

    count = iter(range(7))
    load = lambda a, b: pltpu.make_async_copy(a, b, in_sem.at[next(count)])
    load_state = [load(state.at[0], ext.at[0, :, own, :])]
    load_regrid = [
        load(a.at[0], b) for a, b in ((interp_index, idx), (interp_weight, wgt), (coupling, cpl), (sea_mask, sea))
    ]
    load_rest = [load(velocity.at[0], vel)]
    load_rest += [load(mixing.at[0], mix)]
    sources = [pltpu.make_async_copy(prev.at[s], src.at[s], src_sem.at[s]) for s in range(steps)]

    def remote(a, b, send, recv, device):
        return pltpu.make_async_remote_copy(
            src_ref=a, dst_ref=b, send_sem=send, recv_sem=recv, device_id=device, device_id_type=MESH
        )

    halo_low, halo_high = pl.ds(PAD - REACH, REACH), pl.ds(PAD + rows, REACH)
    to_before, to_after, to_west, to_east, to_ocean = [], [], [], [], []
    for s in range(steps):
        to_before.append(remote(lat_out.at[s, 0], lat_in.at[s, 0], lat_send.at[s, 0], lat_recv.at[s, 0], before))
        to_after.append(remote(lat_out.at[s, 1], lat_in.at[s, 1], lat_send.at[s, 1], lat_recv.at[s, 1], after))
        to_west.append(remote(lon_out.at[s], lon_in.at[s, 0], lon_send.at[s, 0], lon_recv.at[s, 0], west))
        to_east.append(remote(lon_out.at[s], lon_in.at[s, 1], lon_send.at[s, 1], lon_recv.at[s, 1], east))
        to_ocean.append(remote(flux.at[s], src.at[s], flux_send.at[s], flux_recv.at[s], partner))

    barrier = pltpu.get_barrier_semaphore()
    for side in (west, east):
        pl.semaphore_signal(barrier, inc=1, device_id=side, device_id_type=MESH)
    for copy in load_state:
        copy.start()

    @pl.when(has_before)
    def _():
        pl.semaphore_signal(barrier, inc=1, device_id=before, device_id_type=MESH)

    @pl.when(has_after)
    def _():
        pl.semaphore_signal(barrier, inc=1, device_id=after, device_id_type=MESH)

    @pl.when(is_ocean)
    def _():
        pl.semaphore_signal(barrier, inc=1, device_id=partner, device_id_type=MESH)

    @pl.when(is_atmosphere)
    def _():
        for copy in sources:
            copy.start()

    for copy in load_regrid + load_rest:
        copy.start()

    lane = lax.broadcasted_iota(jnp.int32, (rows, cols), 1)

    def pack(packed, level, x):
        turned = pltpu.roll(x, (4 * level + REACH) % cols, 1)
        return jnp.where((lane >= 4 * level) & (lane < 4 * level + 4), turned, packed)

    def pack_lat(s, level, x):
        lat_out[s, 0, pl.ds(REACH * level, REACH), :] = x[:REACH]
        lat_out[s, 1, pl.ds(REACH * level, REACH), :] = x[rows - REACH :]

    for copy in load_state:
        copy.wait()
    packed = jnp.zeros((rows, cols), jnp.float32)
    for level in range(levels):
        x = ext[0, level, own, :]
        packed = pack(packed, level, x)
        pack_lat(0, level, x)
    lon_out[0] = packed
    nothing = jnp.zeros((steps, levels, REACH, cols), jnp.float32)

    @pl.when(jnp.logical_not(has_before))
    def _():
        ext[:, :, halo_low, :] = nothing

    @pl.when(jnp.logical_not(has_after))
    def _():
        ext[:, :, halo_high, :] = nothing

    edges = has_before.astype(jnp.int32) + has_after.astype(jnp.int32)
    pl.semaphore_wait(barrier, 2 + edges + is_atmosphere.astype(jnp.int32))

    def send_halo(s):
        @pl.when(has_before)
        def _():
            to_before[s].start()

        @pl.when(has_after)
        def _():
            to_after[s].start()

        to_west[s].start()
        to_east[s].start()

    send_halo(0)
    for copy in load_regrid:
        copy.wait()
    rate = cpl[...] * sea[...].astype(jnp.float32)

    @pl.when(is_atmosphere)
    def _():
        sources[0].wait()
        flux[0] = rate * (regrid(src.at[0], idx, wgt) - ext[0, 0, own, :])
        to_ocean[0].start()

    for copy in load_rest:
        copy.wait()
    east_speed, north_speed = vel[0] * (1.0 / 12.0), vel[1] * (1.0 / 12.0)
    centre = 1.0 - 4.0 * SMOOTHING
    lon_m2, lon_m1 = -east_speed, SMOOTHING + 8.0 * east_speed
    lon_p1, lon_p2 = SMOOTHING - 8.0 * east_speed, east_speed
    lat_m2, lat_m1 = -north_speed, SMOOTHING + 8.0 * north_speed
    lat_p1, lat_p2 = SMOOTHING - 8.0 * north_speed, north_speed
    own_m2, own_m1 = jnp.where(lane < 2, 0.0, lon_m2), jnp.where(lane < 1, 0.0, lon_m1)
    own_p1 = jnp.where(lane >= cols - 1, 0.0, lon_p1)
    own_p2 = jnp.where(lane >= cols - 2, 0.0, lon_p2)
    place = lax.bitwise_and(lane, 3)
    rim = lax.bitwise_and(place + (cols - REACH), cols - 1)
    spread = lambda c, keep: jnp.where(keep, lane_gather(c, rim), 0.0)
    rim_p2 = spread(lon_p2, place < 2)
    rim_p1 = spread(lon_p1, place == 1)
    rim_m2 = spread(lon_m2, place >= 2)
    rim_m1 = spread(lon_m1, place == 2)
    on_rim = (lane < REACH) | (lane >= cols - REACH)

    inverse, ratio = [None] * levels, [None] * levels
    for level in range(levels - 1, -1, -1):
        pivot = 1.0
        if level < levels - 1:
            pivot = pivot + mix[level] * (1.0 - ratio[level + 1])
        if level > 0:
            pivot = pivot + mix[level - 1]
        inverse[level] = 1.0 / pivot
        if level > 0:
            ratio[level] = mix[level - 1] * inverse[level]
    carry = [mix[level] * inverse[level] for level in range(levels - 1)]

    def own_part(s):
        for level in range(levels):
            x = ext[s, level, own, :]
            y[level] = (
                centre * x
                + own_m2 * pltpu.roll(x, 2, 1)
                + own_m1 * pltpu.roll(x, 1, 1)
                + own_p1 * pltpu.roll(x, cols - 1, 1)
                + own_p2 * pltpu.roll(x, cols - 2, 1)
            )

    for s in range(steps):
        own_part(s)
        if s + 1 < steps:

            @pl.when(is_atmosphere)
            def _():
                sources[s + 1].wait()
                part[s + 1] = regrid(src.at[s + 1], idx, wgt)

        @pl.when(is_ocean)
        def _():
            to_ocean[s].wait_recv()
            part[s] = rate * regrid(src.at[s], idx, wgt)

        @pl.when(has_after)
        def _():
            to_before[s].wait_recv()
            for level in range(levels):
                ext[s, level, halo_high, :] = lat_in[s, 0, pl.ds(REACH * level, REACH), :]

        @pl.when(has_before)
        def _():
            to_after[s].wait_recv()
            for level in range(levels):
                ext[s, level, halo_low, :] = lat_in[s, 1, pl.ds(REACH * level, REACH), :]

        to_west[s].wait_recv()
        to_east[s].wait_recv()
        from_east, from_west = lon_in[s, 0], lon_in[s, 1]
        rims = (
            rim_p2 * pltpu.roll(from_east, cols - 2, 1)
            + rim_p1 * pltpu.roll(from_east, cols - 1, 1)
            + rim_m2 * pltpu.roll(from_west, 2, 1)
            + rim_m1 * pltpu.roll(from_west, 1, 1)
        )
        values = [None] * levels
        for level in range(levels - 1, -1, -1):
            total = (
                y[level]
                + lat_m2 * ext[s, level, pl.ds(PAD - 2, rows), :]
                + lat_m1 * ext[s, level, pl.ds(PAD - 1, rows), :]
                + lat_p1 * ext[s, level, pl.ds(PAD + 1, rows), :]
                + lat_p2 * ext[s, level, pl.ds(PAD + 2, rows), :]
                + jnp.where(on_rim, pltpu.roll(rims, (cols - REACH - 4 * level) % cols, 1), 0.0)
            )
            values[level] = total * inverse[level]
            if level < levels - 1:
                values[level] = values[level] + carry[level] * values[level + 1]

        forcing = jnp.where(is_atmosphere, flux[s], part[s])
        x = values[0] + forcing * inverse[0]
        series[0, s] = jnp.where(is_atmosphere, forcing, x)
        last = s + 1 == steps
        if not last:

            @pl.when(is_atmosphere)
            def _():
                flux[s + 1] = rate * (part[s + 1] - x)
                to_ocean[s + 1].start()

        packed = jnp.zeros((rows, cols), jnp.float32)
        for level in range(levels):
            if level > 0:
                x = values[level] + ratio[level] * x
            if last:
                new_state[0, level] = x
            else:
                ext[s + 1, level, own, :] = x
                packed = pack(packed, level, x)
                pack_lat(s + 1, level, x)
        if not last:
            lon_out[s + 1] = packed
            send_halo(s + 1)

    for s in range(steps):

        @pl.when(is_atmosphere)
        def _():
            to_ocean[s].wait_send()

        @pl.when(has_before)
        def _():
            to_before[s].wait_send()

        @pl.when(has_after)
        def _():
            to_after[s].wait_send()

        to_west[s].wait_send()
        to_east[s].wait_send()


def hand_over(state_in, series_in, state_out, series_out, sem):
    levels = state_in.shape[1]
    group = pl.cdiv(levels, GROUPS)
    copies = [pltpu.make_async_copy(series_in, series_out, sem.at[GROUPS])]
    for i, first in enumerate(range(0, levels, group)):
        some = pl.ds(first, min(group, levels - first))
        copies.append(pltpu.make_async_copy(state_in.at[0, some], state_out.at[0, some], sem.at[i]))
    for copy in copies:
        copy.start()
    for copy in copies:
        copy.wait()


def per_device(n_lat, n_lon, state, prev, mixing, velocity, coupling, sea_mask, index, weight):
    levels, rows, cols = state.shape[1:]
    steps, points = prev.shape[0], index.shape[1]
    tile = (rows, cols)
    floats = lambda *lead: pltpu.VMEM(lead + tile, jnp.float32)
    dma = pltpu.SemaphoreType.DMA
    shapes = (
        jax.ShapeDtypeStruct(state.shape, jnp.float32),
        jax.ShapeDtypeStruct((1, steps) + tile, jnp.float32),
    )
    outs = pl.pallas_call(
        functools.partial(kernel, (n_lat, n_lon, steps, levels, rows, cols)),
        out_shape=tuple(pltpu.VMEM(s.shape, s.dtype) for s in shapes),
        in_specs=[pl.BlockSpec(memory_space=pltpu.HBM)] * 8,
        out_specs=[pl.BlockSpec(memory_space=pltpu.VMEM)] * 2,
        scratch_shapes=[
            pltpu.VMEM((steps, levels, rows + 2 * PAD, cols), jnp.float32),
            floats(steps),
            floats(levels - 1),
            floats(2),
            floats(),
            pltpu.VMEM(tile, jnp.int32),
            pltpu.VMEM((points,) + tile, jnp.int32),
            floats(points),
            floats(steps),
            floats(steps),
            floats(levels),
            pltpu.VMEM((steps, 2, levels * REACH, cols), jnp.float32),
            pltpu.VMEM((steps, 2, levels * REACH, cols), jnp.float32),
            floats(steps),
            floats(steps, 2),
            dma((7,)),
            dma((steps,)),
            dma((steps, 2)),
            dma((steps, 2)),
            dma((steps, 2)),
            dma((steps, 2)),
            dma((steps,)),
            dma((steps,)),
        ],
        compiler_params=pltpu.CompilerParams(collective_id=0, has_side_effects=True, vmem_limit_bytes=VMEM_BYTES),
        name="coupled_window",
    )(*(pltpu.with_memory_space_constraint(a, pltpu.HBM) for a in (state, prev, mixing, velocity, coupling, sea_mask, index, weight)))
    return pl.pallas_call(
        hand_over,
        out_shape=shapes,
        in_specs=[pl.BlockSpec(memory_space=pltpu.VMEM)] * 2,
        out_specs=[pl.BlockSpec(memory_space=pl.ANY)] * 2,
        scratch_shapes=[dma((GROUPS + 1,))],
        compiler_params=pltpu.CompilerParams(vmem_limit_bytes=VMEM_BYTES),
        name="hand_over",
    )(*outs)


def solution(mesh):
    in_specs = (
        P("comp", None, "lat", "lon"),
        P(None, "lat", "lon"),
        P("comp", None, "lat", "lon"),
        P("comp", None, "lat", "lon"),
        P("comp", "lat", "lon"),
        P("comp", "lat", "lon"),
        P("comp", None, "lat", "lon"),
        P("comp", None, "lat", "lon"),
    )
    out_specs = (P("comp", None, "lat", "lon"), P("comp", None, "lat", "lon"))
    return jax.shard_map(
        functools.partial(per_device, mesh.shape["lat"], mesh.shape["lon"]),
        mesh=mesh,
        in_specs=in_specs,
        out_specs=out_specs,
        check_vma=False,
    )
```

```python
import functools

import jax
import jax.numpy as jnp
from jax import lax
from jax.experimental import pallas as pl
from jax.experimental.pallas import tpu as pltpu
from jax.sharding import PartitionSpec as P

SMOOTHING = 0.15
MESH = pl.DeviceIdType.MESH
PAD = 8
REACH = 2
VMEM_BYTES = 8 * 2**20
GROUPS = 4
SUB = 8


def lane_gather(values, lanes):
    return jnp.take_along_axis(values, lanes, axis=1, mode="promise_in_bounds")


def regrid(source, index, weight):
    points, rows, cols = index.shape
    shift = cols.bit_length() - 1
    parts = []
    for top in range(0, rows, SUB):
        total = jnp.zeros((SUB, cols), jnp.float32)
        for j in range(points):
            where = index[j, top : top + SUB, :]
            lanes, owner = lax.bitwise_and(where, cols - 1), lax.shift_right_logical(where, shift)
            picked = jnp.zeros((SUB, cols), jnp.float32)
            for row in range(rows):
                line = jnp.broadcast_to(source[row : row + 1, :], (SUB, cols))
                picked = jnp.where(owner == row, lane_gather(line, lanes), picked)
            total = total + weight[j, top : top + SUB, :] * picked
        parts.append(total)
    return jnp.concatenate(parts, axis=0)


def kernel(
    sizes,
    state,
    prev,
    mixing,
    velocity,
    coupling,
    sea_mask,
    interp_index,
    interp_weight,
    new_state,
    series,
    ext,
    src,
    mix,
    vel,
    cpl,
    sea,
    idx,
    wgt,
    part,
    flux,
    y,
    lat_out,
    lat_in,
    lon_out,
    lon_in,
    in_sem,
    src_sem,
    lat_send,
    lat_recv,
    lon_send,
    lon_recv,
    flux_send,
    flux_recv,
):
    n_lat, n_lon, steps, levels, rows, cols = sizes
    comp, lat, lon = (lax.axis_index(a) for a in ("comp", "lat", "lon"))
    is_atmosphere = comp == 0
    is_ocean = comp != 0
    has_before = lat > 0
    has_after = lat < n_lat - 1
    before, after = {"lat": lat - 1}, {"lat": lat + 1}
    west, east = {"lon": lax.rem(lon + n_lon - 1, n_lon)}, {"lon": lax.rem(lon + 1, n_lon)}
    partner = {"comp": 1 - comp}
    own = pl.ds(PAD, rows)

    count = iter(range(7))
    load = lambda a, b: pltpu.make_async_copy(a, b, in_sem.at[next(count)])
    load_state = [load(state.at[0], ext.at[0, :, own, :])]
    load_regrid = [
        load(a.at[0], b) for a, b in ((interp_index, idx), (interp_weight, wgt), (coupling, cpl), (sea_mask, sea))
    ]
    load_rest = [load(velocity.at[0], vel)]
    load_rest += [load(mixing.at[0], mix)]
    sources = [pltpu.make_async_copy(prev.at[s], src.at[s], src_sem.at[s]) for s in range(steps)]

    def remote(a, b, send, recv, device):
        return pltpu.make_async_remote_copy(
            src_ref=a, dst_ref=b, send_sem=send, recv_sem=recv, device_id=device, device_id_type=MESH
        )

    halo_low, halo_high = pl.ds(PAD - REACH, REACH), pl.ds(PAD + rows, REACH)
    to_before, to_after, to_west, to_east, to_ocean = [], [], [], [], []
    for s in range(steps):
        if s == 0:
            rows_low = (state.at[0, :, pl.ds(0, REACH), :], ext.at[0, :, halo_high, :])
            rows_high = (state.at[0, :, pl.ds(rows - REACH, REACH), :], ext.at[0, :, halo_low, :])
        else:
            rows_low = (lat_out.at[s, 0], lat_in.at[s, 0])
            rows_high = (lat_out.at[s, 1], lat_in.at[s, 1])
        to_before.append(remote(*rows_low, lat_send.at[s, 0], lat_recv.at[s, 0], before))
        to_after.append(remote(*rows_high, lat_send.at[s, 1], lat_recv.at[s, 1], after))
        to_west.append(remote(lon_out.at[s], lon_in.at[s, 0], lon_send.at[s, 0], lon_recv.at[s, 0], west))
        to_east.append(remote(lon_out.at[s], lon_in.at[s, 1], lon_send.at[s, 1], lon_recv.at[s, 1], east))
        to_ocean.append(remote(flux.at[s], src.at[s], flux_send.at[s], flux_recv.at[s], partner))

    barrier = pltpu.get_barrier_semaphore()
    for side in (west, east):
        pl.semaphore_signal(barrier, inc=1, device_id=side, device_id_type=MESH)
    for copy in load_state:
        copy.start()

    @pl.when(has_before)
    def _():
        pl.semaphore_signal(barrier, inc=1, device_id=before, device_id_type=MESH)

    @pl.when(has_after)
    def _():
        pl.semaphore_signal(barrier, inc=1, device_id=after, device_id_type=MESH)

    @pl.when(is_ocean)
    def _():
        pl.semaphore_signal(barrier, inc=1, device_id=partner, device_id_type=MESH)

    @pl.when(is_atmosphere)
    def _():
        for copy in sources:
            copy.start()

    for copy in load_regrid + load_rest:
        copy.start()

    lane = lax.broadcasted_iota(jnp.int32, (rows, cols), 1)

    def pack(packed, level, x):
        turned = pltpu.roll(x, (4 * level + REACH) % cols, 1)
        return jnp.where((lane >= 4 * level) & (lane < 4 * level + 4), turned, packed)

    def pack_lat(s, level, x):
        lat_out[s, 0, pl.ds(REACH * level, REACH), :] = x[:REACH]
        lat_out[s, 1, pl.ds(REACH * level, REACH), :] = x[rows - REACH :]

    edges = has_before.astype(jnp.int32) + has_after.astype(jnp.int32)
    pl.semaphore_wait(barrier, 2 + edges + is_atmosphere.astype(jnp.int32))

    def send_lat(s):
        @pl.when(has_before)
        def _():
            to_before[s].start()

        @pl.when(has_after)
        def _():
            to_after[s].start()

    def send_lon(s):
        to_west[s].start()
        to_east[s].start()

    send_lat(0)
    for copy in load_state:
        copy.wait()
    packed = jnp.zeros((rows, cols), jnp.float32)
    for level in range(levels):
        x = ext[0, level, own, :]
        packed = pack(packed, level, x)
    lon_out[0] = packed
    nothing = jnp.zeros((steps, levels, REACH, cols), jnp.float32)

    @pl.when(jnp.logical_not(has_before))
    def _():
        ext[:, :, halo_low, :] = nothing

    @pl.when(jnp.logical_not(has_after))
    def _():
        ext[:, :, halo_high, :] = nothing

    send_lon(0)
    for copy in load_regrid:
        copy.wait()
    rate = cpl[...] * sea[...].astype(jnp.float32)

    @pl.when(is_atmosphere)
    def _():
        sources[0].wait()
        flux[0] = rate * (regrid(src.at[0], idx, wgt) - ext[0, 0, own, :])
        to_ocean[0].start()

    for copy in load_rest:
        copy.wait()
    east_speed, north_speed = vel[0] * (1.0 / 12.0), vel[1] * (1.0 / 12.0)
    centre = 1.0 - 4.0 * SMOOTHING
    lon_m2, lon_m1 = -east_speed, SMOOTHING + 8.0 * east_speed
    lon_p1, lon_p2 = SMOOTHING - 8.0 * east_speed, east_speed
    lat_m2, lat_m1 = -north_speed, SMOOTHING + 8.0 * north_speed
    lat_p1, lat_p2 = SMOOTHING - 8.0 * north_speed, north_speed
    own_m2, own_m1 = jnp.where(lane < 2, 0.0, lon_m2), jnp.where(lane < 1, 0.0, lon_m1)
    own_p1 = jnp.where(lane >= cols - 1, 0.0, lon_p1)
    own_p2 = jnp.where(lane >= cols - 2, 0.0, lon_p2)
    place = lax.bitwise_and(lane, 3)
    rim = lax.bitwise_and(place + (cols - REACH), cols - 1)
    spread = lambda c, keep: jnp.where(keep, lane_gather(c, rim), 0.0)
    rim_p2 = spread(lon_p2, place < 2)
    rim_p1 = spread(lon_p1, place == 1)
    rim_m2 = spread(lon_m2, place >= 2)
    rim_m1 = spread(lon_m1, place == 2)
    on_rim = (lane < REACH) | (lane >= cols - REACH)

    inverse, ratio = [None] * levels, [None] * levels
    for level in range(levels - 1, -1, -1):
        pivot = 1.0
        if level < levels - 1:
            pivot = pivot + mix[level] * (1.0 - ratio[level + 1])
        if level > 0:
            pivot = pivot + mix[level - 1]
        inverse[level] = 1.0 / pivot
        if level > 0:
            ratio[level] = mix[level - 1] * inverse[level]
    carry = [mix[level] * inverse[level] for level in range(levels - 1)]

    def own_part(s):
        for level in range(levels):
            x = ext[s, level, own, :]
            y[level] = (
                centre * x
                + own_m2 * pltpu.roll(x, 2, 1)
                + own_m1 * pltpu.roll(x, 1, 1)
                + own_p1 * pltpu.roll(x, cols - 1, 1)
                + own_p2 * pltpu.roll(x, cols - 2, 1)
            )

    for s in range(steps):
        own_part(s)
        if s + 1 < steps:

            @pl.when(is_atmosphere)
            def _():
                sources[s + 1].wait()
                part[s + 1] = regrid(src.at[s + 1], idx, wgt)

        @pl.when(is_ocean)
        def _():
            to_ocean[s].wait_recv()
            part[s] = rate * regrid(src.at[s], idx, wgt)

        @pl.when(has_after)
        def _():
            to_before[s].wait_recv()
            for level in range(levels if s > 0 else 0):
                ext[s, level, halo_high, :] = lat_in[s, 0, pl.ds(REACH * level, REACH), :]

        @pl.when(has_before)
        def _():
            to_after[s].wait_recv()
            for level in range(levels if s > 0 else 0):
                ext[s, level, halo_low, :] = lat_in[s, 1, pl.ds(REACH * level, REACH), :]

        to_west[s].wait_recv()
        to_east[s].wait_recv()
        from_east, from_west = lon_in[s, 0], lon_in[s, 1]
        rims = (
            rim_p2 * pltpu.roll(from_east, cols - 2, 1)
            + rim_p1 * pltpu.roll(from_east, cols - 1, 1)
            + rim_m2 * pltpu.roll(from_west, 2, 1)
            + rim_m1 * pltpu.roll(from_west, 1, 1)
        )
        values = [None] * levels
        for level in range(levels - 1, -1, -1):
            total = (
                y[level]
                + lat_m2 * ext[s, level, pl.ds(PAD - 2, rows), :]
                + lat_m1 * ext[s, level, pl.ds(PAD - 1, rows), :]
                + lat_p1 * ext[s, level, pl.ds(PAD + 1, rows), :]
                + lat_p2 * ext[s, level, pl.ds(PAD + 2, rows), :]
                + jnp.where(on_rim, pltpu.roll(rims, (cols - REACH - 4 * level) % cols, 1), 0.0)
            )
            values[level] = total * inverse[level]
            if level < levels - 1:
                values[level] = values[level] + carry[level] * values[level + 1]

        forcing = jnp.where(is_atmosphere, flux[s], part[s])
        x = values[0] + forcing * inverse[0]
        series[0, s] = jnp.where(is_atmosphere, forcing, x)
        last = s + 1 == steps
        if not last:

            @pl.when(is_atmosphere)
            def _():
                flux[s + 1] = rate * (part[s + 1] - x)
                to_ocean[s + 1].start()

        packed = jnp.zeros((rows, cols), jnp.float32)
        for level in range(levels):
            if level > 0:
                x = values[level] + ratio[level] * x
            if last:
                new_state[0, level] = x
            else:
                ext[s + 1, level, own, :] = x
                packed = pack(packed, level, x)
                pack_lat(s + 1, level, x)
        if not last:
            lon_out[s + 1] = packed
            send_lat(s + 1)
            send_lon(s + 1)

    for s in range(steps):

        @pl.when(is_atmosphere)
        def _():
            to_ocean[s].wait_send()

        @pl.when(has_before)
        def _():
            to_before[s].wait_send()

        @pl.when(has_after)
        def _():
            to_after[s].wait_send()

        to_west[s].wait_send()
        to_east[s].wait_send()


def hand_over(state_in, series_in, state_out, series_out, sem):
    levels = state_in.shape[1]
    group = pl.cdiv(levels, GROUPS)
    copies = [pltpu.make_async_copy(series_in, series_out, sem.at[GROUPS])]
    for i, first in enumerate(range(0, levels, group)):
        some = pl.ds(first, min(group, levels - first))
        copies.append(pltpu.make_async_copy(state_in.at[0, some], state_out.at[0, some], sem.at[i]))
    for copy in copies:
        copy.start()
    for copy in copies:
        copy.wait()


def per_device(n_lat, n_lon, state, prev, mixing, velocity, coupling, sea_mask, index, weight):
    levels, rows, cols = state.shape[1:]
    steps, points = prev.shape[0], index.shape[1]
    tile = (rows, cols)
    floats = lambda *lead: pltpu.VMEM(lead + tile, jnp.float32)
    dma = pltpu.SemaphoreType.DMA
    shapes = (
        jax.ShapeDtypeStruct(state.shape, jnp.float32),
        jax.ShapeDtypeStruct((1, steps) + tile, jnp.float32),
    )
    outs = pl.pallas_call(
        functools.partial(kernel, (n_lat, n_lon, steps, levels, rows, cols)),
        out_shape=tuple(pltpu.VMEM(s.shape, s.dtype) for s in shapes),
        in_specs=[pl.BlockSpec(memory_space=pltpu.HBM)] * 8,
        out_specs=[pl.BlockSpec(memory_space=pltpu.VMEM)] * 2,
        scratch_shapes=[
            pltpu.VMEM((steps, levels, rows + 2 * PAD, cols), jnp.float32),
            floats(steps),
            floats(levels - 1),
            floats(2),
            floats(),
            pltpu.VMEM(tile, jnp.int32),
            pltpu.VMEM((points,) + tile, jnp.int32),
            floats(points),
            floats(steps),
            floats(steps),
            floats(levels),
            pltpu.VMEM((steps, 2, levels * REACH, cols), jnp.float32),
            pltpu.VMEM((steps, 2, levels * REACH, cols), jnp.float32),
            floats(steps),
            floats(steps, 2),
            dma((7,)),
            dma((steps,)),
            dma((steps, 2)),
            dma((steps, 2)),
            dma((steps, 2)),
            dma((steps, 2)),
            dma((steps,)),
            dma((steps,)),
        ],
        compiler_params=pltpu.CompilerParams(collective_id=0, has_side_effects=True, vmem_limit_bytes=VMEM_BYTES),
        name="coupled_window",
    )(*(pltpu.with_memory_space_constraint(a, pltpu.HBM) for a in (state, prev, mixing, velocity, coupling, sea_mask, index, weight)))
    return pl.pallas_call(
        hand_over,
        out_shape=shapes,
        in_specs=[pl.BlockSpec(memory_space=pltpu.VMEM)] * 2,
        out_specs=[pl.BlockSpec(memory_space=pl.ANY)] * 2,
        scratch_shapes=[dma((GROUPS + 1,))],
        compiler_params=pltpu.CompilerParams(vmem_limit_bytes=VMEM_BYTES),
        name="hand_over",
    )(*outs)


def solution(mesh):
    in_specs = (
        P("comp", None, "lat", "lon"),
        P(None, "lat", "lon"),
        P("comp", None, "lat", "lon"),
        P("comp", None, "lat", "lon"),
        P("comp", "lat", "lon"),
        P("comp", "lat", "lon"),
        P("comp", None, "lat", "lon"),
        P("comp", None, "lat", "lon"),
    )
    out_specs = (P("comp", None, "lat", "lon"), P("comp", None, "lat", "lon"))
    return jax.shard_map(
        functools.partial(per_device, mesh.shape["lat"], mesh.shape["lon"]),
        mesh=mesh,
        in_specs=in_specs,
        out_specs=out_specs,
        check_vma=False,
    )
```
